128 devices in a mesh: cand: 8 (over y, core), hist: 16 (over z, x).
Axes of the slice: x: 4, y: 4, z: 4, core: 2. Of those that a mesh axis runs over, the one named last changes fastest.
Arguments:
- cand_x: bfloat16 [512, 128, 1024], P(('cand', 'hist')), may hold values from -6 to 6
- w_query: bfloat16 [1024, 1024], replicated, may hold values from -0.1875 to 0.1875
- w_gate: bfloat16 [1024, 1024], replicated, may hold values from -0.1875 to 0.1875
- w_out: bfloat16 [1024, 1024], replicated, may hold values from -0.1875 to 0.1875
- history_kv: bfloat16 [16, 48, 128, 2048], P('cand', 'hist')
- tile_user: int32 [512], P('cand'), may hold values from 0 to 15, as said below
- user_row: int32 [16], replicated, may hold values from 0 to 15, as said below
- hist_len: int32 [16], replicated, may hold values from 1 to 6144, as said below
- pattern: int32 [512, 48], P('cand', 'hist'), may hold values 0 or 1
Outputs:
- mixed: bfloat16 [512, 128, 1024], P(('cand', 'hist'))
The draws below stay inside these ranges and needn't reach their ends.
Inputs may be any that keep to these rules, and one draw needn't show every extreme that they name: `tile_user`: the tiles of each index of cand (64 consecutive tiles) name, among the 2 cache rows of each index of cand (rows k * 2 to k * 2 + 1 for index k), exactly 1. `user_row`: each cache row is used by exactly one user. `hist_len`: some user has exactly 6144 actions.
All inputs are finite; a program needn't handle non-finite values. No bound on the sum of `pattern` on one device may be relied on, other than what follows from the above.
Results may differ from the reference program's by a relative error of at most 0.013.
Values may be sent and summed in bfloat16 or wider, within the bound.
A program may use at most 192 MiB of HBM per device.

```python
import math
import jax
import jax.numpy as jnp
from jax import lax

D = 1024
H = 8
DH = 128
BLK = 128
NB = 48
UQ = 1
UC = 2
TD = 4
USERS = 16
TILES = 512
N_CAND = 8
N_HIST = 16


def route_helper(key):
    key_perm, key_pick, key_extra, key_shuffle = jax.random.split(key, 4)
    row_of_user = jax.random.permutation(key_perm, USERS).astype(jnp.int32)
    user_of_row = jnp.argsort(row_of_user).astype(jnp.int32)
    pick_keys = jax.random.split(key_pick, N_CAND * N_CAND)
    chosen_local = jax.vmap(lambda sub_key: jax.random.permutation(sub_key, UC)[:UQ])(pick_keys).astype(jnp.int32)
    owners = jnp.tile(jnp.arange(N_CAND, dtype=jnp.int32), N_CAND)
    allowed_rows = (owners[:, None] * UC + chosen_local).reshape(N_CAND, N_CAND * UQ)
    group_tiles = TD * N_HIST
    allowed_count = N_CAND * UQ
    extra_slots = jax.random.randint(key_extra, (N_CAND, group_tiles), 0, allowed_count, dtype=jnp.int32)
    tile_positions = jnp.arange(group_tiles, dtype=jnp.int32)[None, :]
    slot_choice = jnp.where(tile_positions < allowed_count, jnp.broadcast_to(tile_positions, (N_CAND, group_tiles)), extra_slots)
    shuffle_keys = jax.random.split(key_shuffle, N_CAND)
    shuffle_order = jax.vmap(lambda sub_key: jax.random.permutation(sub_key, group_tiles))(shuffle_keys).astype(jnp.int32)
    slot_choice = jnp.take_along_axis(slot_choice, shuffle_order, axis=1)
    tile_rows = jnp.take_along_axis(allowed_rows, slot_choice, axis=1).reshape(N_CAND * group_tiles)
    return (row_of_user, user_of_row[tile_rows].astype(jnp.int32))


def draw_user_row(key, part):
    return route_helper(key)[0]


def draw_tile_user(key, part):
    return route_helper(key)[1]


def draw_history_kv(key, part):
    key = jax.random.fold_in(key, 11)
    key_first, key_second, key_columns = jax.random.split(key, 3)
    shape = (USERS, NB, BLK, D)
    column_scale = jnp.exp(jax.random.uniform(key_columns, (D,), jnp.float32, math.log(0.3), math.log(3.0)))
    key_part = jnp.clip(jax.random.normal(key_first, shape, jnp.float32), -6.0, 6.0)
    value_part = jnp.clip(jax.random.normal(key_second, shape, jnp.float32), -6.0, 6.0) * column_scale
    return jnp.concatenate([key_part, value_part], axis=-1).astype(jnp.bfloat16)


def draw_hist_len(key, part):
    key = jax.random.fold_in(key, 23)
    key_length, key_longest = jax.random.split(key)
    lengths = jax.random.randint(key_length, (USERS,), 1, NB * BLK + 1, dtype=jnp.int32)
    longest = jax.random.randint(key_longest, (), 0, USERS, dtype=jnp.int32)
    return jnp.where(jnp.arange(USERS, dtype=jnp.int32) == longest, NB * BLK, lengths).astype(jnp.int32)


def with_ends(result, stream_key, smallest, high):
    longest = result.shape.index(max(result.shape))
    spots = []
    for shift in (0, 1):
        where = [jax.random.randint(jax.random.fold_in(stream_key, axis), (), 0, length) for axis, length in enumerate(result.shape)]
        where[longest] = (where[longest] + shift) % result.shape[longest]
        spots.append(tuple(where))
    return result.at[spots[0]].set(smallest).at[spots[1]].set(high)


def steps_of(own_key, extent, cuts, low, high):
    gain = 1.0
    for axis_at, blocks in cuts:
        steps = jax.random.uniform(jax.random.fold_in(jax.random.fold_in(own_key, 6), axis_at), (blocks,), jnp.float32, low / len(cuts), high / len(cuts))
        gain = gain * jnp.repeat(jnp.exp(steps), extent[axis_at] // blocks).reshape((-1,) + (1,) * (len(extent) - 1 - axis_at))
    return gain


def scatter_about(rng, shape, deviation, most, cuts=(), held_as=jnp.bfloat16):
    values = jax.random.normal(rng, shape, jnp.float32) * deviation
    if len(cuts) > 0:
        values = steps_of(rng, shape, cuts, -0.22, 0.18) * values
    return jnp.clip(values, min=-most, max=most).astype(held_as)


def setup_inputs(seed: int = 0) -> dict:
    key_of = jax.random.split(jax.random.key(seed), 10)
    cand_x = scatter_about(key_of[0], (TILES, BLK, D), 1.0, 6.0, ((0, 128),))
    w_query = scatter_about(key_of[1], (D, D), D ** -0.5, 0.1875)
    w_gate = scatter_about(key_of[2], (D, D), D ** -0.5, 0.1875)
    w_out = scatter_about(key_of[3], (D, D), D ** -0.5, 0.1875)
    history_kv = draw_history_kv(jax.random.fold_in(key_of[9], 71), 0)
    tile_user = draw_tile_user(jax.random.fold_in(key_of[9], 71), 0)
    user_row = draw_user_row(jax.random.fold_in(key_of[9], 71), 0)
    hist_len = draw_hist_len(jax.random.fold_in(key_of[9], 71), 0)
    pattern = with_ends((jax.random.randint(key_of[8], (TILES, NB), 0, 4) < 3).astype(jnp.int32), jax.random.fold_in(key_of[8], 1), 0, 1)
    return {"cand_x": cand_x, "w_query": w_query, "w_gate": w_gate, "w_out": w_out, "history_kv": history_kv, "tile_user": tile_user, "user_row": user_row, "hist_len": hist_len, "pattern": pattern}


norm_epsilon = 1e-05

def reference(cand_x, w_query, w_gate, w_out, history_kv, tile_user, user_row, hist_len, pattern):
    flat_rows = cand_x.reshape(TILES * BLK, D)
    queries = jax.nn.silu(jnp.dot(flat_rows, w_query, preferred_element_type=jnp.float32)).astype(jnp.bfloat16)
    gate_act = jax.nn.silu(jnp.dot(flat_rows, w_gate, preferred_element_type=jnp.float32)).astype(jnp.bfloat16)
    queries = queries.reshape(TILES, BLK, H, DH)
    group_blocks = NB // N_HIST
    positions = jnp.arange(NB * BLK, dtype=jnp.int32)
    score_scale = 1.0 / DH ** 0.5

    def one_tile(tile_index):
        user_id = tile_user[tile_index]
        cache_row = user_row[user_id]
        length = hist_len[user_id]
        user_cache = history_kv[cache_row].reshape(NB * BLK, 2, H, DH).astype(jnp.float32)
        key_rows = user_cache[:, 0]
        value_rows = user_cache[:, 1]
        q_tile = queries[tile_index].astype(jnp.float32)
        scores = jnp.einsum('chd,thd->hct', q_tile, key_rows) * score_scale
        block_mask = jnp.broadcast_to(pattern[tile_index][:, None], (NB, BLK)).reshape(NB * BLK)
        allowed = (positions < length) & (block_mask > 0)
        weights = jnp.where(allowed[None, None, :], jax.nn.silu(scores), 0.0) / length.astype(jnp.float32)
        weights = lax.optimization_barrier(weights.astype(jnp.bfloat16)).astype(jnp.float32)
        weights = weights.reshape(H, BLK, N_HIST, group_blocks * BLK)
        grouped_values = value_rows.reshape(N_HIST, group_blocks * BLK, H, DH)
        per_group = jnp.einsum('hcgt,gthd->gchd', weights, grouped_values)
        per_group = lax.optimization_barrier(per_group.astype(jnp.bfloat16)).astype(jnp.float32)
        return lax.optimization_barrier(jnp.sum(per_group, axis=0)).reshape(BLK, D)
    attention = lax.map(one_tile, jnp.arange(TILES, dtype=jnp.int32))
    mean_square = lax.optimization_barrier(jnp.mean(attention * attention, axis=-1, keepdims=True))
    normed = attention * lax.rsqrt(mean_square + norm_epsilon)
    hidden = (normed * gate_act.reshape(TILES, BLK, D).astype(jnp.float32)).astype(jnp.bfloat16)
    mixed = jnp.dot(hidden.reshape(TILES * BLK, D), w_out, preferred_element_type=jnp.float32) + flat_rows.astype(jnp.float32)
    return mixed.astype(jnp.bfloat16).reshape(TILES, BLK, D)
```

```python
import functools

import jax
import jax.numpy as jnp
from jax import lax
from jax.experimental import pallas as pl
from jax.experimental.pallas import tpu as pltpu
from jax.sharding import PartitionSpec as P

DH = 128
CHUNKS = 2

norm_epsilon = 1e-05


def attend_kernel(order_ref, row_ref, q_ref, k_ref, v_ref, m_ref, o_ref, *, heads, span):
    del order_ref, row_ref
    half_scale = 0.5 / DH**0.5
    open_over_length = m_ref[0]
    for h in range(heads):
        cols = slice(h * DH, (h + 1) * DH)
        keys = k_ref[0, :, :, cols].reshape(span, DH)
        values = v_ref[0, :, :, cols].reshape(span, DH)
        half = (
            lax.dot_general(
                q_ref[0, :, cols],
                keys,
                (((1,), (1,)), ((), ())),
                preferred_element_type=jnp.float32,
            )
            * half_scale
        )
        weights = ((half + half * jnp.tanh(half)) * open_over_length).astype(jnp.bfloat16)
        out = jnp.dot(weights, values, preferred_element_type=jnp.float32)
        o_ref[0, :, cols] = out.astype(jnp.bfloat16)


def attend(order, sorted_rows, q_tiles, cache, open_over_length):
    tile_count, block_len, width = q_tiles.shape
    blocks_here = cache.shape[1]
    span = blocks_here * block_len
    kernel = functools.partial(attend_kernel, heads=width // DH, span=span)
    return pl.pallas_call(
        kernel,
        grid_spec=pltpu.PrefetchScalarGridSpec(
            num_scalar_prefetch=2,
            grid=(tile_count,),
            in_specs=[
                pl.BlockSpec((1, block_len, width), lambda i, order, rows: (order[i], 0, 0)),
                pl.BlockSpec((1, blocks_here, block_len, width), lambda i, order, rows: (rows[i], 0, 0, 0)),
                pl.BlockSpec((1, blocks_here, block_len, width), lambda i, order, rows: (rows[i], 0, 0, 1)),
                pl.BlockSpec((1, 1, span), lambda i, order, rows: (order[i], 0, 0)),
            ],
            out_specs=pl.BlockSpec((1, block_len, width), lambda i, order, rows: (order[i], 0, 0)),
        ),
        out_shape=jax.ShapeDtypeStruct(q_tiles.shape, jnp.bfloat16),
        cost_estimate=pl.CostEstimate(
            flops=4 * tile_count * block_len * span * width,
            bytes_accessed=4 * tile_count * block_len * width + 2 * cache.size,
            transcendentals=tile_count * block_len * span * (width // DH),
        ),
        compiler_params=pltpu.CompilerParams(vmem_limit_bytes=24 * 1024 * 1024),
    )(order, sorted_rows, q_tiles, cache, cache, open_over_length)


def per_device(cand_x, w_query, w_gate, w_out, history_kv, tile_user, user_row, hist_len, pattern):
    tiles_here, block_len, model_width = cand_x.shape
    blocks_here = history_kv.shape[1]
    span = blocks_here * block_len
    width = model_width // CHUNKS

    caches = []
    for c in range(CHUNKS):
        part = jnp.concatenate(
            [
                history_kv[..., c * width : (c + 1) * width],
                history_kv[..., model_width + c * width : model_width + (c + 1) * width],
            ],
            axis=-1,
        )
        caches.append(lax.all_gather(part, "cand", axis=0, tiled=True))

    flat_rows = cand_x.reshape(tiles_here * block_len, model_width)
    queries = jax.nn.silu(jnp.dot(flat_rows, w_query, preferred_element_type=jnp.float32)).astype(
        jnp.bfloat16
    )
    queries = queries.reshape(tiles_here, block_len, model_width)
    q_parts = [
        lax.all_gather(queries[..., c * width : (c + 1) * width], "hist", axis=0, tiled=True)
        for c in range(CHUNKS)
    ]
    gate_act = jax.nn.silu(jnp.dot(flat_rows, w_gate, preferred_element_type=jnp.float32)).astype(
        jnp.bfloat16
    )

    tile_count = tile_user.shape[0]
    rows_named = user_row[tile_user]
    lengths = hist_len[tile_user]
    tile_ids = jnp.arange(tile_count, dtype=jnp.int32)
    before = (rows_named[None, :] < rows_named[:, None]) | (
        (rows_named[None, :] == rows_named[:, None]) & (tile_ids[None, :] < tile_ids[:, None])
    )
    rank = jnp.sum(before.astype(jnp.int32), axis=1)
    placed = (rank[None, :] == tile_ids[:, None]).astype(jnp.int32)
    order = jnp.sum(placed * tile_ids[None, :], axis=1)
    sorted_rows = jnp.sum(placed * rows_named[None, :], axis=1)

    positions = lax.axis_index("hist") * span + jnp.arange(span, dtype=jnp.int32)
    block_open = jnp.broadcast_to(
        pattern[:, :, None], (tile_count, blocks_here, block_len)
    ).reshape(tile_count, span)
    allowed = (positions[None, :] < lengths[:, None]) & (block_open > 0)
    open_over_length = jnp.where(allowed, 1.0 / lengths.astype(jnp.float32)[:, None], 0.0)[:, None, :]

    sums = []
    for c in range(CHUNKS):
        partial = attend(order, sorted_rows, q_parts[c], caches[c], open_over_length)
        sums.append(lax.psum_scatter(partial, "hist", scatter_dimension=0, tiled=True))
    attention = jnp.concatenate(sums, axis=-1).astype(jnp.float32)
    attention = attention.reshape(tiles_here * block_len, model_width)
    mean_square = jnp.mean(attention * attention, axis=-1, keepdims=True)
    normed = attention * lax.rsqrt(mean_square + norm_epsilon)
    hidden = (normed * gate_act.astype(jnp.float32)).astype(jnp.bfloat16)
    mixed = jnp.dot(hidden, w_out, preferred_element_type=jnp.float32) + flat_rows.astype(
        jnp.float32
    )
    return mixed.astype(jnp.bfloat16).reshape(tiles_here, block_len, model_width)


def solution(mesh):
    return jax.shard_map(
        per_device,
        mesh=mesh,
        in_specs=(
            P(("cand", "hist"), None, None),
            P(),
            P(),
            P(),
            P("cand", "hist", None, None),
            P("cand"),
            P(),
            P(),
            P("cand", "hist"),
        ),
        out_specs=P(("cand", "hist"), None, None),
        check_vma=False,
    )
```

```python
import functools

import jax
import jax.numpy as jnp
from jax import lax
from jax.experimental import pallas as pl
from jax.experimental.pallas import tpu as pltpu
from jax.sharding import PartitionSpec as P

DH = 128
RING = 4
CORES = 2
QUAD = 4
MESH = pl.DeviceIdType.MESH
DIRECT_QUERIES = (0, 1)
DIRECT_SUMS = (6, 7)

norm_epsilon = 1e-05


STEPS = (
    ("kv_own", "kv_next", "kv_far", "q_own", "q_next", "q_line", "q_line_next")
    + ("compute0", "compute1", "compute2", "rs_one", "rs_two", "rs_three", "rs_four", "rs_five")
    + ("route", "gate_load", "gate")
)
ORDER = (
    24, 0, 25, 1, 26, 27, 28, 40, 41, 35, 29, 36, 8, 120, 9, 2,
    34, 48, 16, 49, 4, 3, 43, 17, 42, 44, 56, 64, 72, 80, 57, 65,
    51, 73, 81, 37, 10, 88, 11, 12, 50, 6, 7, 18, 89, 5, 52, 45,
    30, 19, 96, 58, 66, 74, 82, 97, 31, 59, 53, 67, 75, 83, 90, 14,
    128, 104, 136, 13, 38, 15, 20, 39, 91, 112, 105, 47, 21, 98, 60, 46,
    68, 113, 76, 84, 99, 106, 61, 69, 77, 85, 92, 54, 23, 55, 22, 93,
    107, 114, 100, 62, 70, 78, 86, 115, 101, 63, 71, 79, 87, 109, 94, 108,
    95, 117, 116, 102, 103, 118, 119,
)


def layer_kernel(
    user_row_ref,
    hist_len_ref,
    tile_user_ref,
    pattern_ref,
    cand_ref,
    w_query_ref,
    w_gate_ref,
    history_ref,
    att_ref,
    gate_ref,
    *scratch,
    heads,
    quads,
    tiles_here,
    block_len,
    model_width,
    span,
):
    scratch = list(scratch)

    def take(count):
        taken = scratch[:count]
        del scratch[:count]
        return taken

    kv = take(heads)
    q = take(heads)
    osort = take(2)
    s1, s2p, s2m, r1a, r1b, r2m, r2p, keep = [take(2) for _ in range(8)]
    t1, t2p, t2m = [take(2) for _ in range(3)]
    u1, u2m, u2p = [take(2 + len(DIRECT_SUMS)) for _ in range(3)]
    x_in, weight, open_ref, table, table_smem = take(5)
    local_sem, send_sem, recv_sem = take(3)

    cand = lax.axis_index("cand")
    hist = lax.axis_index("hist")
    y, core = cand // CORES, cand % CORES
    z, x = hist // RING, hist % RING
    xp, xm, xo = (x + 1) % RING, (x + RING - 1) % RING, (x + 2) % RING
    zp, zm, zo = (z + 1) % RING, (z + RING - 1) % RING, (z + 2) % RING
    yp, ym, yo = [((y + d) % RING) * CORES + core for d in (1, RING - 1, 2)]
    dev_yp, dev_ym = (yp, hist), (ym, hist)
    dev_sib = (y * CORES + (CORES - 1 - core), hist)
    dev_xp, dev_xm = (cand, z * RING + xp), (cand, z * RING + xm)
    dev_zp, dev_zm = (cand, zp * RING + x), (cand, zm * RING + x)

    dev_xo, dev_zo = (cand, z * RING + xo), (cand, zo * RING + x)

    barrier = pltpu.get_barrier_semaphore()
    everyone = (dev_yp, dev_ym, dev_sib, dev_xp, dev_xm, dev_xo, dev_zp, dev_zm, dev_zo)
    for device in everyone:
        pl.semaphore_signal(barrier, inc=1, device_id=device, device_id_type=MESH)

    sends = {}
    per_head = 24

    def remote(src, dst, key, device):
        name, h = key
        number = h * per_head + KEYS.index(name)
        return pltpu.make_async_remote_copy(
            src_ref=src,
            dst_ref=dst,
            send_sem=send_sem.at[number],
            recv_sem=recv_sem.at[number],
            device_id=device,
            device_id_type=MESH,
        )

    def send(src, dst, name, h, device):
        copy = remote(src, dst, (name, h), device)
        copy.start()
        sends[(name, h)] = copy

    def arrive(dst, name, h):
        remote(dst, dst, (name, h), dev_sib).wait_recv()

    def sent(name, h):
        copy = sends.pop((name, h), None)
        if copy is not None:
            copy.wait_send()

    def own_copies(h):
        cols = pl.ds(h * DH, DH)
        value_cols = pl.ds((heads + h) * DH, DH)
        rows = 2
        copies = []
        for k, columns in enumerate((cols, value_cols)):
            copies.append(
                pltpu.make_async_copy(
                    history_ref.at[:, :, columns],
                    kv[h].at[pl.ds(cand * rows, rows), k],
                    local_sem.at[h * 2 + k],
                )
            )
        return copies

    def fetch(src, dst, number):
        return pltpu.make_async_copy(src, dst, local_sem.at[2 * heads + number])

    fetched = [
        fetch(cand_ref, x_in, 0),
        fetch(w_query_ref, weight, 1),
        fetch(w_gate_ref, weight, 2),
        fetch(table, table_smem, 3),
    ]
    fetched[0].start()
    fetched[1].start()
    own = [own_copies(h) for h in range(heads)]
    for h in range(heads):
        for copy in own[h]:
            copy.start()
    fetched[0].wait()
    fetched[1].wait()

    def silu(v):
        return 0.5 * v + 0.5 * v * jnp.tanh(0.5 * v)

    def project(first, width):
        rows = x_in[...].reshape(tiles_here * block_len, model_width)
        product = jnp.dot(
            rows, weight[:, first : first + width], preferred_element_type=jnp.float32
        )
        return silu(product).astype(jnp.bfloat16)

    def project_pair(h):
        both = project(h * DH, 2 * DH)
        for n in range(2):
            mine = both[:, n * DH : (n + 1) * DH].reshape(tiles_here, block_len, DH)
            q[h + n][z, pl.ds(x * tiles_here, tiles_here)] = mine

    project_pair(0)
    pl.semaphore_wait(barrier, len(everyone))

    def gate_load(h):
        fetched[2].start()

    def gate(h):
        fetched[2].wait()
        width = 2 * DH
        for first in range(0, model_width, width):
            gate_ref[:, :, first : first + width] = project(first, width).reshape(
                tiles_here, block_len, width
            )

    def route(h):
        tile_count = tile_user_ref.shape[1]
        i32 = jnp.int32
        tile_user = tile_user_ref[...]
        rows = jnp.zeros_like(tile_user)
        lengths = jnp.zeros_like(tile_user)
        for user in range(user_row_ref.shape[0]):
            hit = tile_user == user
            rows = jnp.where(hit, user_row_ref[user], rows)
            lengths = jnp.where(hit, hist_len_ref[user], lengths)
        square = (tile_count, tile_count)
        down, along = lax.broadcasted_iota(i32, square, 0), lax.broadcasted_iota(i32, square, 1)

        def column(v):
            return jnp.sum(
                jnp.where(down == along, jnp.broadcast_to(v, square), 0), axis=1, keepdims=True
            )

        rank = jnp.sum(
            jnp.where((column(rows) == rows) & (down < along), 1, 0), axis=0, keepdims=True
        )
        row_ids = lax.broadcasted_iota(i32, (user_row_ref.shape[0], tile_count), 0)
        count = jnp.sum(jnp.where(row_ids == rows, 1, 0), axis=1, keepdims=True)
        need = lax.shift_right_logical(count + (QUAD - 1), jnp.full_like(count, 2))
        first = jnp.sum(jnp.where(row_ids < rows, need, 0), axis=0, keepdims=True)
        tile_slot = QUAD * first + rank
        wide = (tile_count, table.shape[1])
        slot_tile = jnp.sum(
            jnp.where(
                column(tile_slot) == lax.broadcasted_iota(i32, wide, 1),
                lax.broadcasted_iota(i32, wide, 0),
                0,
            ),
            axis=0,
            keepdims=True,
        )
        table[...] = jnp.zeros_like(table)
        table[0:1, :] = slot_tile
        table[1:2, 0:tile_count] = tile_slot
        table[2:3, 0:tile_count] = rows
        fetched[3].start()
        positions = hist * span + lax.broadcasted_iota(i32, (tile_count, span), 1)
        pattern = pattern_ref[...]
        block_open = jnp.concatenate(
            [
                jnp.broadcast_to(pattern[:, b : b + 1], (tile_count, block_len))
                for b in range(pattern.shape[1])
            ],
            axis=1,
        )
        length = jnp.broadcast_to(column(lengths), (tile_count, span))
        allowed = (positions < length) & (block_open > 0)
        open_ref[...] = jnp.where(allowed, 1.0 / length.astype(jnp.float32), 0.0)
        fetched[3].wait()

    def pair_of(owner):
        return pl.ds(owner * 2, 2)

    other = 1 - 2 * core

    def kv_own(h):
        own[h][0].wait()
        own[h][1].wait()
        mine = kv[h].at[pair_of(cand)]
        send(mine, mine, "kv+", h, dev_yp)
        send(mine, mine, "kv-", h, dev_ym)
        send(mine, mine, "kvs0", h, dev_sib)

    def kv_next(h):
        below, above = kv[h].at[pair_of(ym)], kv[h].at[pair_of(yp)]
        arrive(below, "kv+", h)
        first = kv[h].at[ym * 2]
        send(first, first, "kvf+", h, dev_yp)
        send(below, below, "kvs1", h, dev_sib)
        arrive(above, "kv-", h)
        second = kv[h].at[yp * 2 + 1]
        send(second, second, "kvf-", h, dev_ym)
        send(above, above, "kvs2", h, dev_sib)

    def kv_far(h):
        arrive(kv[h].at[yo * 2], "kvf+", h)
        arrive(kv[h].at[yo * 2 + 1], "kvf-", h)
        far = kv[h].at[pair_of(yo)]
        send(far, far, "kvs3", h, dev_sib)

    def kv_ready(h):
        for number, owner in enumerate((cand, ym, yp, yo)):
            arrive(kv[h].at[pair_of(owner + other)], "kvs%d" % number, h)

    def slot(h, zz, xx, start=0, size=tiles_here):
        return q[h].at[zz, pl.ds(xx * tiles_here + start, size)]

    half = tiles_here // 2

    def q_own(h):
        if h % 2 == 0 and h > 0:
            project_pair(h)
        mine = slot(h, z, x)
        first = h % 2 == 0
        send(mine, mine, "q+", h, dev_xp if first else dev_zp)
        send(mine, mine, "q-", h, dev_xm if first else dev_zm)
        if h in DIRECT_QUERIES:
            send(mine, mine, "qf+", h, dev_xo if first else dev_zo)

    def q_next(h):
        if h % 2 == 0:
            low, high, dp, dm = (z, xm), (z, xp), dev_xp, dev_xm
        else:
            low, high, dp, dm = (zm, x), (zp, x), dev_zp, dev_zm
        arrive(slot(h, *low), "q+", h)
        part = slot(h, *low, 0, half)
        send(part, part, "qf+", h, dp)
        arrive(slot(h, *high), "q-", h)
        part = slot(h, *high, half, half)
        send(part, part, "qf-", h, dm)

    def line(h, at, part=None):
        if h % 2 == 0:
            width = RING * tiles_here
            begin, size = {None: (0, width), 0: (0, width // 2), 1: (width // 2, width // 2)}[part]
            return q[h].at[at, pl.ds(begin, size)]
        begin, size = {None: (0, RING), 0: (0, RING // 2), 1: (RING // 2, RING // 2)}[part]
        return q[h].at[pl.ds(begin, size), pl.ds(at * tiles_here, tiles_here)]

    def q_line(h):
        first = h % 2 == 0
        far = (z, xo) if first else (zo, x)
        if h in DIRECT_QUERIES:
            arrive(slot(h, *((z, xm) if first else (zm, x))), "q+", h)
            arrive(slot(h, *((z, xp) if first else (zp, x))), "q-", h)
            arrive(slot(h, *far), "qf+", h)
        else:
            arrive(slot(h, *far, 0, half), "qf+", h)
            arrive(slot(h, *far, half, half), "qf-", h)
        at, dp, dm = (z, dev_zp, dev_zm) if h % 2 == 0 else (x, dev_xp, dev_xm)
        mine = line(h, at)
        send(mine, mine, "l+", h, dp)
        send(mine, mine, "l-", h, dm)

    def q_line_next(h):
        low, high, dp, dm = (zm, zp, dev_zp, dev_zm) if h % 2 == 0 else (xm, xp, dev_xp, dev_xm)
        arrive(line(h, low), "l+", h)
        part = line(h, low, 0)
        send(part, part, "lf+", h, dp)
        arrive(line(h, high), "l-", h)
        part = line(h, high, 1)
        send(part, part, "lf-", h, dm)

    def q_ready(h):
        far = zo if h % 2 == 0 else xo
        arrive(line(h, far, 0), "lf+", h)
        arrive(line(h, far, 1), "lf-", h)

    half_scale = 0.5 / DH**0.5

    def quad(h, number):
        tiles = [table_smem[0, number * QUAD + a] for a in range(QUAD)]
        row = table_smem[2, tiles[0]]
        group = RING * tiles_here
        block = jnp.concatenate([q[h][t // group, t % group] for t in tiles], axis=0)
        scores = lax.dot_general(
            block, kv[h][row, 0], (((1,), (1,)), ((), ())), preferred_element_type=jnp.float32
        )
        weights = []
        for a in range(QUAD):
            part = (scores[a * DH : (a + 1) * DH] * half_scale).astype(jnp.bfloat16)
            weights.append((part + part * jnp.tanh(part)) * open_ref[pl.ds(tiles[a], 1), :].astype(jnp.bfloat16))
        out = jnp.dot(
            jnp.concatenate(weights, axis=0), kv[h][row, 1], preferred_element_type=jnp.float32
        ).astype(jnp.bfloat16)
        for a in range(QUAD):
            osort[h % 2][number * QUAD + a] = out[a * DH : (a + 1) * DH]

    third = (quads + 2) // 3
    cuts = (0, third, 2 * third, quads)
    unroll = 4

    def compute(part, h):
        if part == 0:
            kv_ready(h)
            q_ready(h)
        first, last = cuts[part], cuts[part + 1]
        whole = (last - first) // unroll

        def body(i, carry):
            for j in range(unroll):
                quad(h, first + i * unroll + j)
            return carry

        lax.fori_loop(0, whole, body, 0)
        for number in range(first + whole * unroll, last):
            quad(h, number)

    def tile_at(h, at, j, i):
        return ((j * RING + at) if h % 2 == 0 else (at * RING + j)) * tiles_here + i

    def partial(h, at, j, i):
        return osort[h % 2][table_smem[1, tile_at(h, at, j, i)]]

    def each_tile(body, first=0, last=RING):
        def step(n, carry):
            for i in range(tiles_here):
                body(n, i)
            return carry

        lax.fori_loop(first, last, step, 0)

    f32 = jnp.float32
    b16 = jnp.bfloat16

    def axis_one(h):
        return (x, xp, xm, xo, dev_xp, dev_xm) if h % 2 == 0 else (z, zp, zm, zo, dev_zp, dev_zm)

    def axis_two(h):
        return axis_one(h + 1)

    def rs_one(h):
        e = h % 2
        at, up, down, far, dp, dm = axis_one(h)
        for name in ("a+", "a-"):
            sent(name, h - 2)

        def body(j, i):
            s1[e][j, i] = partial(h, far, j, i)

        each_tile(body)
        send(s1[e].at[pl.ds(0, 2)], r1a[e], "a+", h, dp)
        send(s1[e].at[pl.ds(2, 2)], r1b[e], "a-", h, dm)

    def rs_two(h):
        e = h % 2
        at, up, down, far, dp, dm = axis_one(h)
        arrive(r1a[e], "a+", h)
        arrive(r1b[e], "a-", h)
        for name in ("b+", "b-"):
            sent(name, h - 2)

        def low(j, i):
            s2p[e][j, i] = (partial(h, up, j, i).astype(f32) + r1a[e][j, i].astype(f32)).astype(b16)
            s2m[e][j, i] = partial(h, down, j, i)

        def high(j, i):
            s2p[e][j, i] = partial(h, up, j, i)
            s2m[e][j, i] = (
                partial(h, down, j, i).astype(f32) + r1b[e][j - 2, i].astype(f32)
            ).astype(b16)

        each_tile(low, 0, 2)
        each_tile(high, 2, 4)
        send(s2p[e], r2m[e], "b+", h, dp)
        send(s2m[e], r2p[e], "b-", h, dm)

    def landing(h):
        return 2 + DIRECT_SUMS.index(h) if h in DIRECT_SUMS else h % 2

    def rs_three(h):
        e = h % 2
        u = landing(h)
        at = axis_one(h)[0]
        _, up, down, far, dp, dm = axis_two(h)
        arrive(r2m[e], "b+", h)
        arrive(r2p[e], "b-", h)
        for name in ("c+", "c-"):
            sent(name, h - 2)

        def body(j, i):
            keep[e][j, i] = (
                partial(h, at, j, i).astype(f32)
                + r2m[e][j, i].astype(f32)
                + r2p[e][j, i].astype(f32)
            ).astype(keep[e].dtype)

        each_tile(body)
        for i in range(tiles_here):
            t1[e][i] = keep[e][far, i].astype(b16)
        if h not in DIRECT_SUMS:
            send(t1[e].at[pl.ds(0, half)], u1[u].at[pl.ds(0, half)], "c+", h, dp)
            send(t1[e].at[pl.ds(half, half)], u1[u].at[pl.ds(half, half)], "c-", h, dm)
            return
        for name in ("d+", "d-"):
            sent(name, h - 2)
        for i in range(tiles_here):
            t2p[e][i] = keep[e][up, i].astype(b16)
            t2m[e][i] = keep[e][down, i].astype(b16)
        send(t2p[e], u2m[u], "d+", h, dp)
        send(t2m[e], u2p[u], "d-", h, dm)
        send(t1[e], u1[u], "c+", h, dev_zo if h % 2 == 0 else dev_xo)

    def rs_four(h):
        e = h % 2
        u = landing(h)
        _, up, down, _, dp, dm = axis_two(h)
        arrive(u1[u].at[pl.ds(0, half)], "c+", h)
        arrive(u1[u].at[pl.ds(half, half)], "c-", h)
        for name in ("d+", "d-"):
            sent(name, h - 2)
        for i in range(tiles_here):
            to_up, to_down = keep[e][up, i].astype(f32), keep[e][down, i].astype(f32)
            if i < half:
                to_up = to_up + u1[u][i].astype(f32)
            else:
                to_down = to_down + u1[u][i].astype(f32)
            t2p[e][i] = to_up.astype(b16)
            t2m[e][i] = to_down.astype(b16)
        send(t2p[e], u2m[u], "d+", h, dp)
        send(t2m[e], u2p[u], "d-", h, dm)

    def rs_five(h):
        e = h % 2
        u = landing(h)
        at = axis_two(h)[0]
        arrive(u2m[u], "d+", h)
        arrive(u2p[u], "d-", h)
        direct = h in DIRECT_SUMS
        if direct:
            arrive(u1[u], "c+", h)
        for i in range(tiles_here):
            total = keep[e][at, i].astype(f32) + u2m[u][i].astype(f32) + u2p[u][i].astype(f32)
            if direct:
                total = total + u1[u][i].astype(f32)
            att_ref[i, :, h * DH : (h + 1) * DH] = total

    run = {
        "kv_own": kv_own,
        "kv_next": kv_next,
        "kv_far": kv_far,
        "q_own": q_own,
        "q_next": q_next,
        "q_line": q_line,
        "q_line_next": q_line_next,
        "compute0": functools.partial(compute, 0),
        "compute1": functools.partial(compute, 1),
        "compute2": functools.partial(compute, 2),
        "rs_one": rs_one,
        "rs_two": rs_two,
        "rs_three": rs_three,
        "rs_four": rs_four,
        "rs_five": rs_five,
        "route": route,
        "gate_load": gate_load,
        "gate": gate,
    }
    for code in ORDER:
        run[STEPS[code // 8]](code % 8)
    for name, h in list(sends):
        sent(name, h)


KEYS = (
    ("kv+", "kv-", "kvf+", "kvf-", "kvs0", "kvs1", "kvs2", "kvs3")
    + ("q+", "q-", "qf+", "qf-", "l+", "l-", "lf+", "lf-")
    + ("a+", "a-", "b+", "b-", "c+", "c-", "d+", "d-")
)


def attend(user_row, hist_len, tile_user, pattern, cand_x, w_query, w_gate, history):
    tiles_here, block_len, model_width = cand_x.shape
    heads = model_width // DH
    tile_count = tile_user.shape[1]
    cache_rows = CORES * RING * history.shape[0]
    quads = (tile_count + (QUAD - 1) * cache_rows // 2) // QUAD
    span = history.shape[1]
    b16 = jnp.bfloat16
    tile = (block_len, DH)
    lines = pltpu.VMEM((RING, tiles_here) + tile, b16)
    half_lines = pltpu.VMEM((RING // 2, tiles_here) + tile, b16)
    few = pltpu.VMEM((tiles_here,) + tile, b16)
    scratch = (
        [pltpu.VMEM((cache_rows, 2, span, DH), b16)] * heads
        + [pltpu.VMEM((RING, RING * tiles_here) + tile, b16)] * heads
        + [pltpu.VMEM((quads * QUAD,) + tile, b16)] * 2
        + [lines] * 2
        + [lines] * 4
        + [half_lines] * 4
        + [lines] * 4
        + [lines] * 2
        + [few] * 6
        + [few] * (6 + 3 * len(DIRECT_SUMS))
        + [
            pltpu.VMEM(cand_x.shape, b16),
            pltpu.VMEM(w_query.shape, b16),
            pltpu.VMEM((tile_count, span), jnp.float32),
            pltpu.VMEM((8, DH), jnp.int32),
            pltpu.SMEM((8, DH), jnp.int32),
            pltpu.SemaphoreType.DMA((heads * 2 + 4,)),
            pltpu.SemaphoreType.DMA((heads * 24,)),
            pltpu.SemaphoreType.DMA((heads * 24,)),
        ]
    )
    smem = pl.BlockSpec(memory_space=pltpu.SMEM)
    vmem = pl.BlockSpec(memory_space=pltpu.VMEM)
    return pl.pallas_call(
        functools.partial(
            layer_kernel,
            heads=heads,
            quads=quads,
            tiles_here=tiles_here,
            block_len=block_len,
            model_width=model_width,
            span=span,
        ),
        in_specs=[smem, smem, vmem, vmem] + [pl.BlockSpec(memory_space=pl.ANY)] * 4,
        out_specs=[vmem, vmem],
        out_shape=[
            jax.ShapeDtypeStruct(cand_x.shape, jnp.float32),
            jax.ShapeDtypeStruct(cand_x.shape, b16),
        ],
        scratch_shapes=scratch,
        cost_estimate=pl.CostEstimate(
            flops=4 * tile_count * block_len * span * model_width,
            bytes_accessed=2 * history.size,
            transcendentals=tile_count * block_len * span * heads,
        ),
        compiler_params=pltpu.CompilerParams(
            collective_id=0, has_side_effects=True, vmem_limit_bytes=63 * 1024 * 1024
        ),
    )(user_row, hist_len, tile_user, pattern, cand_x, w_query, w_gate, history)


def per_device(cand_x, w_query, w_gate, w_out, history_kv, tile_user, user_row, hist_len, pattern):
    tiles_here, block_len, model_width = cand_x.shape
    own_rows, blocks_here, _, kv_width = history_kv.shape
    span = blocks_here * block_len
    history = history_kv.reshape(own_rows, span, kv_width)

    attention, gate_act = attend(
        user_row, hist_len, tile_user[None, :], pattern, cand_x, w_query, w_gate, history
    )
    flat_rows = cand_x.reshape(tiles_here * block_len, model_width)
    gate_act = gate_act.reshape(tiles_here * block_len, model_width)
    attention = attention.reshape(tiles_here * block_len, model_width)
    mean_square = jnp.mean(attention * attention, axis=-1, keepdims=True)
    normed = attention * lax.rsqrt(mean_square + norm_epsilon)
    hidden = (normed * gate_act.astype(jnp.float32)).astype(jnp.bfloat16)
    mixed = jnp.dot(hidden, w_out, preferred_element_type=jnp.float32) + flat_rows.astype(
        jnp.float32
    )
    return mixed.astype(jnp.bfloat16).reshape(tiles_here, block_len, model_width)


def solution(mesh):
    return jax.shard_map(
        per_device,
        mesh=mesh,
        in_specs=(
            P(("cand", "hist"), None, None),
            P(),
            P(),
            P(),
            P("cand", "hist", None, None),
            P("cand"),
            P(),
            P(),
            P("cand", "hist"),
        ),
        out_specs=P(("cand", "hist"), None, None),
        check_vma=False,
    )
```

```python
import functools

import jax
import jax.numpy as jnp
from jax import lax
from jax.experimental import pallas as pl
from jax.experimental.pallas import tpu as pltpu
from jax.sharding import PartitionSpec as P

DH = 128
RING = 4
CORES = 2
QUAD = 4
MESH = pl.DeviceIdType.MESH
DIRECT_QUERIES = ()
DIRECT_SUMS = (7,)

norm_epsilon = 1e-05


STEPS = (
    ("kv_own", "kv_next", "kv_far", "q_own", "q_next", "q_line", "q_line_next")
    + ("compute0", "compute1", "compute2", "rs_one", "rs_two", "rs_three", "rs_four", "rs_five")
    + ("route", "gate_load", "gate")
)
ORDER = (
    24, 25, 0, 26, 27, 32, 33, 1, 28, 29, 34, 40, 41, 8, 36, 30,
    128, 35, 9, 37, 48, 16, 49, 3, 2, 120, 42, 17, 43, 4, 44, 56,
    64, 72, 80, 57, 51, 65, 73, 81, 88, 45, 10, 50, 11, 5, 12, 38,
    89, 31, 52, 18, 6, 7, 136, 19, 96, 58, 66, 74, 82, 97, 59, 67,
    39, 53, 75, 83, 90, 105, 13, 14, 20, 104, 91, 112, 22, 21, 47, 15,
    98, 60, 68, 46, 76, 113, 99, 84, 61, 69, 106, 107, 77, 85, 92, 54,
    23, 93, 114, 115, 55, 100, 62, 70, 78, 86, 101, 63, 71, 79, 87, 94,
    108, 95, 116, 102, 109, 117, 103, 110, 118, 119,
)


def layer_kernel(
    user_row_ref,
    hist_len_ref,
    tile_user_ref,
    pattern_ref,
    cand_ref,
    w_query_ref,
    w_gate_ref,
    w_out_ref,
    history_ref,
    mixed_ref,
    *scratch,
    heads,
    quads,
    tiles_here,
    block_len,
    model_width,
    span,
):
    scratch = list(scratch)

    def take(count):
        taken = scratch[:count]
        del scratch[:count]
        return taken

    kv = take(heads)
    q = take(heads)
    osort = take(2)
    s1, s2p, s2m, r1a, r1b, r2m, r2p, keep = [take(2) for _ in range(8)]
    t1, t2p, t2m = [take(2) for _ in range(3)]
    u1, u2m, u2p = [take(2 + len(DIRECT_SUMS)) for _ in range(3)]
    x_in, weight, gate_act, mixing, squares, open_ref, table, table_smem = take(8)
    local_sem, send_sem, recv_sem = take(3)

    cand = lax.axis_index("cand")
    hist = lax.axis_index("hist")
    y, core = cand // CORES, cand % CORES
    z, x = hist // RING, hist % RING
    xp, xm, xo = (x + 1) % RING, (x + RING - 1) % RING, (x + 2) % RING
    zp, zm, zo = (z + 1) % RING, (z + RING - 1) % RING, (z + 2) % RING
    yp, ym, yo = [((y + d) % RING) * CORES + core for d in (1, RING - 1, 2)]
    dev_yp, dev_ym = (yp, hist), (ym, hist)
    dev_sib = (y * CORES + (CORES - 1 - core), hist)
    dev_xp, dev_xm = (cand, z * RING + xp), (cand, z * RING + xm)
    dev_zp, dev_zm = (cand, zp * RING + x), (cand, zm * RING + x)

    dev_xo, dev_zo = (cand, z * RING + xo), (cand, zo * RING + x)

    barrier = pltpu.get_barrier_semaphore()
    everyone = (dev_yp, dev_ym, dev_sib, dev_xp, dev_xm, dev_xo, dev_zp, dev_zm, dev_zo)
    for device in everyone:
        pl.semaphore_signal(barrier, inc=1, device_id=device, device_id_type=MESH)

    sends = {}
    per_head = 24

    def remote(src, dst, key, device):
        name, h = key
        number = h * per_head + KEYS.index(name)
        return pltpu.make_async_remote_copy(
            src_ref=src,
            dst_ref=dst,
            send_sem=send_sem.at[number],
            recv_sem=recv_sem.at[number],
            device_id=device,
            device_id_type=MESH,
        )

    def send(src, dst, name, h, device):
        copy = remote(src, dst, (name, h), device)
        copy.start()
        sends[(name, h)] = copy

    def arrive(dst, name, h):
        remote(dst, dst, (name, h), dev_sib).wait_recv()

    def sent(name, h):
        copy = sends.pop((name, h), None)
        if copy is not None:
            copy.wait_send()

    def own_copies(h):
        cols = pl.ds(h * DH, DH)
        value_cols = pl.ds((heads + h) * DH, DH)
        rows = 2
        copies = []
        for k, columns in enumerate((cols, value_cols)):
            copies.append(
                pltpu.make_async_copy(
                    history_ref.at[:, :, columns],
                    kv[h].at[pl.ds(cand * rows, rows), k],
                    local_sem.at[h * 2 + k],
                )
            )
        return copies

    def fetch(src, dst, number):
        return pltpu.make_async_copy(src, dst, local_sem.at[2 * heads + number])

    fetched = [
        fetch(cand_ref, x_in, 0),
        fetch(w_query_ref, weight, 1),
        fetch(w_gate_ref, weight, 2),
        fetch(table, table_smem, 3),
        fetch(w_out_ref, weight, 4),
    ]
    fetched[0].start()
    fetched[1].start()
    own = [own_copies(h) for h in range(heads)]
    for h in range(heads):
        for copy in own[h]:
            copy.start()
    fetched[0].wait()
    fetched[1].wait()

    def silu(v):
        return 0.5 * v + 0.5 * v * jnp.tanh(0.5 * v)

    def project(first, width):
        rows = x_in[...].reshape(tiles_here * block_len, model_width)
        product = jnp.dot(
            rows, weight[:, first : first + width], preferred_element_type=jnp.float32
        )
        return silu(product).astype(jnp.bfloat16)

    def project_pair(h):
        both = project(h * DH, 2 * DH)
        for n in range(2):
            mine = both[:, n * DH : (n + 1) * DH].reshape(tiles_here, block_len, DH)
            q[h + n][z, pl.ds(x * tiles_here, tiles_here)] = mine

    project_pair(0)
    pl.semaphore_wait(barrier, len(everyone))

    def gate_load(h):
        fetched[2].start()

    def gate(h):
        fetched[2].wait()
        width = 2 * DH
        for first in range(0, model_width, width):
            gate_act[:, first : first + width] = project(first, width)
        fetched[4].start()

    def route(h):
        tile_count = tile_user_ref.shape[1]
        i32 = jnp.int32
        tile_user = tile_user_ref[...]
        rows = jnp.zeros_like(tile_user)
        lengths = jnp.zeros_like(tile_user)
        for user in range(user_row_ref.shape[0]):
            hit = tile_user == user
            rows = jnp.where(hit, user_row_ref[user], rows)
            lengths = jnp.where(hit, hist_len_ref[user], lengths)
        square = (tile_count, tile_count)
        down, along = lax.broadcasted_iota(i32, square, 0), lax.broadcasted_iota(i32, square, 1)

        def column(v):
            return jnp.sum(
                jnp.where(down == along, jnp.broadcast_to(v, square), 0), axis=1, keepdims=True
            )

        rank = jnp.sum(
            jnp.where((column(rows) == rows) & (down < along), 1, 0), axis=0, keepdims=True
        )
        row_ids = lax.broadcasted_iota(i32, (user_row_ref.shape[0], tile_count), 0)
        count = jnp.sum(jnp.where(row_ids == rows, 1, 0), axis=1, keepdims=True)
        need = lax.shift_right_logical(count + (QUAD - 1), jnp.full_like(count, 2))
        first = jnp.sum(jnp.where(row_ids < rows, need, 0), axis=0, keepdims=True)
        tile_slot = QUAD * first + rank
        wide = (tile_count, table.shape[1])
        slot_tile = jnp.sum(
            jnp.where(
                column(tile_slot) == lax.broadcasted_iota(i32, wide, 1),
                lax.broadcasted_iota(i32, wide, 0),
                0,
            ),
            axis=0,
            keepdims=True,
        )
        table[...] = jnp.zeros_like(table)
        table[0:1, :] = slot_tile
        table[1:2, 0:tile_count] = tile_slot
        table[2:3, 0:tile_count] = rows
        fetched[3].start()
        positions = hist * span + lax.broadcasted_iota(i32, (tile_count, span), 1)
        pattern = pattern_ref[...]
        block_open = jnp.concatenate(
            [
                jnp.broadcast_to(column(pattern[b : b + 1, :]), (tile_count, block_len))
                for b in range(pattern.shape[0])
            ],
            axis=1,
        )
        length = jnp.broadcast_to(column(lengths), (tile_count, span))
        allowed = (positions < length) & (block_open > 0)
        open_ref[...] = jnp.where(allowed, 1.0 / length.astype(jnp.float32), 0.0)
        fetched[3].wait()

    def pair_of(owner):
        return pl.ds(owner * 2, 2)

    other = 1 - 2 * core

    def kv_own(h):
        own[h][0].wait()
        own[h][1].wait()
        mine = kv[h].at[pair_of(cand)]
        send(mine, mine, "kv+", h, dev_yp)
        send(mine, mine, "kv-", h, dev_ym)
        send(mine, mine, "kvs0", h, dev_sib)

    def kv_next(h):
        below, above = kv[h].at[pair_of(ym)], kv[h].at[pair_of(yp)]
        arrive(below, "kv+", h)
        first = kv[h].at[ym * 2]
        send(first, first, "kvf+", h, dev_yp)
        send(below, below, "kvs1", h, dev_sib)
        arrive(above, "kv-", h)
        second = kv[h].at[yp * 2 + 1]
        send(second, second, "kvf-", h, dev_ym)
        send(above, above, "kvs2", h, dev_sib)

    def kv_far(h):
        arrive(kv[h].at[yo * 2], "kvf+", h)
        arrive(kv[h].at[yo * 2 + 1], "kvf-", h)
        far = kv[h].at[pair_of(yo)]
        send(far, far, "kvs3", h, dev_sib)

    def kv_ready(h):
        for number, owner in enumerate((cand, ym, yp, yo)):
            arrive(kv[h].at[pair_of(owner + other)], "kvs%d" % number, h)

    def slot(h, zz, xx, start=0, size=tiles_here):
        return q[h].at[zz, pl.ds(xx * tiles_here + start, size)]

    half = tiles_here // 2

    def q_own(h):
        if h % 2 == 0 and h > 0:
            project_pair(h)
        mine = slot(h, z, x)
        first = h % 2 == 0
        send(mine, mine, "q+", h, dev_xp if first else dev_zp)
        send(mine, mine, "q-", h, dev_xm if first else dev_zm)
        if h in DIRECT_QUERIES:
            send(mine, mine, "qf+", h, dev_xo if first else dev_zo)

    def q_next(h):
        if h % 2 == 0:
            low, high, dp, dm = (z, xm), (z, xp), dev_xp, dev_xm
        else:
            low, high, dp, dm = (zm, x), (zp, x), dev_zp, dev_zm
        arrive(slot(h, *low), "q+", h)
        part = slot(h, *low, 0, half)
        send(part, part, "qf+", h, dp)
        arrive(slot(h, *high), "q-", h)
        part = slot(h, *high, half, half)
        send(part, part, "qf-", h, dm)

    def line(h, at, part=None):
        if h % 2 == 0:
            width = RING * tiles_here
            begin, size = {None: (0, width), 0: (0, width // 2), 1: (width // 2, width // 2)}[part]
            return q[h].at[at, pl.ds(begin, size)]
        begin, size = {None: (0, RING), 0: (0, RING // 2), 1: (RING // 2, RING // 2)}[part]
        return q[h].at[pl.ds(begin, size), pl.ds(at * tiles_here, tiles_here)]

    def q_line(h):
        first = h % 2 == 0
        far = (z, xo) if first else (zo, x)
        if h in DIRECT_QUERIES:
            arrive(slot(h, *((z, xm) if first else (zm, x))), "q+", h)
            arrive(slot(h, *((z, xp) if first else (zp, x))), "q-", h)
            arrive(slot(h, *far), "qf+", h)
        else:
            arrive(slot(h, *far, 0, half), "qf+", h)
            arrive(slot(h, *far, half, half), "qf-", h)
        at, dp, dm = (z, dev_zp, dev_zm) if h % 2 == 0 else (x, dev_xp, dev_xm)
        mine = line(h, at)
        send(mine, mine, "l+", h, dp)
        send(mine, mine, "l-", h, dm)

    def q_line_next(h):
        low, high, dp, dm = (zm, zp, dev_zp, dev_zm) if h % 2 == 0 else (xm, xp, dev_xp, dev_xm)
        arrive(line(h, low), "l+", h)
        part = line(h, low, 0)
        send(part, part, "lf+", h, dp)
        arrive(line(h, high), "l-", h)
        part = line(h, high, 1)
        send(part, part, "lf-", h, dm)

    def q_ready(h):
        far = zo if h % 2 == 0 else xo
        arrive(line(h, far, 0), "lf+", h)
        arrive(line(h, far, 1), "lf-", h)

    half_scale = 0.5 / DH**0.5

    def quad(h, number):
        tiles = [table_smem[0, number * QUAD + a] for a in range(QUAD)]
        row = table_smem[2, tiles[0]]
        group = RING * tiles_here
        block = jnp.concatenate([q[h][t // group, t % group] for t in tiles], axis=0)
        scores = lax.dot_general(
            block, kv[h][row, 0], (((1,), (1,)), ((), ())), preferred_element_type=jnp.float32
        )
        weights = []
        for a in range(QUAD):
            part = (scores[a * DH : (a + 1) * DH] * half_scale).astype(jnp.bfloat16)
            weights.append((part + part * jnp.tanh(part)) * open_ref[pl.ds(tiles[a], 1), :].astype(jnp.bfloat16))
        out = jnp.dot(
            jnp.concatenate(weights, axis=0), kv[h][row, 1], preferred_element_type=jnp.float32
        ).astype(jnp.bfloat16)
        for a in range(QUAD):
            osort[h % 2][number * QUAD + a] = out[a * DH : (a + 1) * DH]

    third = (quads + 2) // 3
    cuts = (0, third, 2 * third, quads)
    unroll = 4

    def compute(part, h):
        if part == 0:
            kv_ready(h)
            q_ready(h)
        first, last = cuts[part], cuts[part + 1]
        whole = (last - first) // unroll

        def body(i, carry):
            for j in range(unroll):
                quad(h, first + i * unroll + j)
            return carry

        lax.fori_loop(0, whole, body, 0)
        for number in range(first + whole * unroll, last):
            quad(h, number)

    def tile_at(h, at, j, i):
        return ((j * RING + at) if h % 2 == 0 else (at * RING + j)) * tiles_here + i

    def partial(h, at, j, i):
        return osort[h % 2][table_smem[1, tile_at(h, at, j, i)]]

    def each_tile(body, first=0, last=RING):
        def step(n, carry):
            for i in range(tiles_here):
                body(n, i)
            return carry

        lax.fori_loop(first, last, step, 0)

    f32 = jnp.float32
    b16 = jnp.bfloat16

    def axis_one(h):
        return (x, xp, xm, xo, dev_xp, dev_xm) if h % 2 == 0 else (z, zp, zm, zo, dev_zp, dev_zm)

    def axis_two(h):
        return axis_one(h + 1)

    def rs_one(h):
        e = h % 2
        at, up, down, far, dp, dm = axis_one(h)
        for name in ("a+", "a-"):
            sent(name, h - 2)

        def body(j, i):
            s1[e][j, i] = partial(h, far, j, i)

        each_tile(body)
        send(s1[e].at[pl.ds(0, 2)], r1a[e], "a+", h, dp)
        send(s1[e].at[pl.ds(2, 2)], r1b[e], "a-", h, dm)

    def rs_two(h):
        e = h % 2
        at, up, down, far, dp, dm = axis_one(h)
        arrive(r1a[e], "a+", h)
        arrive(r1b[e], "a-", h)
        for name in ("b+", "b-"):
            sent(name, h - 2)

        def low(j, i):
            s2p[e][j, i] = (partial(h, up, j, i).astype(f32) + r1a[e][j, i].astype(f32)).astype(b16)
            s2m[e][j, i] = partial(h, down, j, i)

        def high(j, i):
            s2p[e][j, i] = partial(h, up, j, i)
            s2m[e][j, i] = (
                partial(h, down, j, i).astype(f32) + r1b[e][j - 2, i].astype(f32)
            ).astype(b16)

        each_tile(low, 0, 2)
        each_tile(high, 2, 4)
        send(s2p[e], r2m[e], "b+", h, dp)
        send(s2m[e], r2p[e], "b-", h, dm)

    def landing(h):
        return 2 + DIRECT_SUMS.index(h) if h in DIRECT_SUMS else h % 2

    def rs_three(h):
        e = h % 2
        u = landing(h)
        at = axis_one(h)[0]
        _, up, down, far, dp, dm = axis_two(h)
        arrive(r2m[e], "b+", h)
        arrive(r2p[e], "b-", h)
        for name in ("c+", "c-"):
            sent(name, h - 2)

        def body(j, i):
            keep[e][j, i] = (
                partial(h, at, j, i).astype(f32)
                + r2m[e][j, i].astype(f32)
                + r2p[e][j, i].astype(f32)
            ).astype(keep[e].dtype)

        each_tile(body)
        for i in range(tiles_here):
            t1[e][i] = keep[e][far, i].astype(b16)
        if h not in DIRECT_SUMS:
            send(t1[e].at[pl.ds(0, half)], u1[u].at[pl.ds(0, half)], "c+", h, dp)
            send(t1[e].at[pl.ds(half, half)], u1[u].at[pl.ds(half, half)], "c-", h, dm)
            return
        for name in ("d+", "d-"):
            sent(name, h - 2)
        for i in range(tiles_here):
            t2p[e][i] = keep[e][up, i].astype(b16)
            t2m[e][i] = keep[e][down, i].astype(b16)
        send(t2p[e], u2m[u], "d+", h, dp)
        send(t2m[e], u2p[u], "d-", h, dm)
        send(t1[e], u1[u], "c+", h, dev_zo if h % 2 == 0 else dev_xo)

    def rs_four(h):
        e = h % 2
        u = landing(h)
        _, up, down, _, dp, dm = axis_two(h)
        arrive(u1[u].at[pl.ds(0, half)], "c+", h)
        arrive(u1[u].at[pl.ds(half, half)], "c-", h)
        for name in ("d+", "d-"):
            sent(name, h - 2)
        for i in range(tiles_here):
            to_up, to_down = keep[e][up, i].astype(f32), keep[e][down, i].astype(f32)
            if i < half:
                to_up = to_up + u1[u][i].astype(f32)
            else:
                to_down = to_down + u1[u][i].astype(f32)
            t2p[e][i] = to_up.astype(b16)
            t2m[e][i] = to_down.astype(b16)
        send(t2p[e], u2m[u], "d+", h, dp)
        send(t2m[e], u2p[u], "d-", h, dm)

    def rs_five(h):
        e = h % 2
        u = landing(h)
        at = axis_two(h)[0]
        arrive(u2m[u], "d+", h)
        arrive(u2p[u], "d-", h)
        direct = h in DIRECT_SUMS
        if direct:
            arrive(u1[u], "c+", h)
        cols = slice(h * DH, (h + 1) * DH)
        total = keep[e][at].astype(f32) + u2m[u][...].astype(f32) + u2p[u][...].astype(f32)
        if direct:
            total = total + u1[u][...].astype(f32)
        total = total.reshape(tiles_here * block_len, DH)
        hidden = (total * gate_act[:, cols].astype(f32)).astype(b16)
        if not mixed_heads:
            fetched[4].wait()
        for first in range(0, model_width, 2 * DH):
            wide = slice(first, first + 2 * DH)
            product = jnp.dot(hidden, weight[cols, wide], preferred_element_type=f32)
            mixing[:, wide] = mixing[:, wide] + product if mixed_heads else product
        squares[...] = squares[...] + total * total if mixed_heads else total * total
        mixed_heads.append(h)

    mixed_heads = []

    def finish():
        mean_square = jnp.sum(squares[...], axis=1, keepdims=True) * (1.0 / model_width)
        scale = lax.rsqrt(mean_square + norm_epsilon)
        for i in range(tiles_here):
            rows = slice(i * block_len, (i + 1) * block_len)
            mixed_ref[i] = (mixing[rows, :] * scale[rows] + x_in[i].astype(f32)).astype(b16)

    run = {
        "kv_own": kv_own,
        "kv_next": kv_next,
        "kv_far": kv_far,
        "q_own": q_own,
        "q_next": q_next,
        "q_line": q_line,
        "q_line_next": q_line_next,
        "compute0": functools.partial(compute, 0),
        "compute1": functools.partial(compute, 1),
        "compute2": functools.partial(compute, 2),
        "rs_one": rs_one,
        "rs_two": rs_two,
        "rs_three": rs_three,
        "rs_four": rs_four,
        "rs_five": rs_five,
        "route": route,
        "gate_load": gate_load,
        "gate": gate,
    }
    for code in ORDER:
        run[STEPS[code // 8]](code % 8)
    finish()
    for name, h in list(sends):
        sent(name, h)


KEYS = (
    ("kv+", "kv-", "kvf+", "kvf-", "kvs0", "kvs1", "kvs2", "kvs3")
    + ("q+", "q-", "qf+", "qf-", "l+", "l-", "lf+", "lf-")
    + ("a+", "a-", "b+", "b-", "c+", "c-", "d+", "d-")
)


def layer(user_row, hist_len, tile_user, pattern, cand_x, w_query, w_gate, w_out, history):
    tiles_here, block_len, model_width = cand_x.shape
    heads = model_width // DH
    tile_count = tile_user.shape[1]
    cache_rows = CORES * RING * history.shape[0]
    quads = (tile_count + (QUAD - 1) * cache_rows // 2) // QUAD
    span = history.shape[1]
    b16 = jnp.bfloat16
    tile = (block_len, DH)
    lines = pltpu.VMEM((RING, tiles_here) + tile, b16)
    half_lines = pltpu.VMEM((RING // 2, tiles_here) + tile, b16)
    few = pltpu.VMEM((tiles_here,) + tile, b16)
    scratch = (
        [pltpu.VMEM((cache_rows, 2, span, DH), b16)] * heads
        + [pltpu.VMEM((RING, RING * tiles_here) + tile, b16)] * heads
        + [pltpu.VMEM((quads * QUAD,) + tile, b16)] * 2
        + [lines] * 2
        + [lines] * 4
        + [half_lines] * 4
        + [lines] * 4
        + [lines] * 2
        + [few] * 6
        + [few] * (6 + 3 * len(DIRECT_SUMS))
        + [
            pltpu.VMEM(cand_x.shape, b16),
            pltpu.VMEM(w_query.shape, b16),
            pltpu.VMEM((tiles_here * block_len, model_width), b16),
            pltpu.VMEM((tiles_here * block_len, model_width), jnp.float32),
            pltpu.VMEM((tiles_here * block_len, DH), jnp.float32),
            pltpu.VMEM((tile_count, span), jnp.float32),
            pltpu.VMEM((8, DH), jnp.int32),
            pltpu.SMEM((8, DH), jnp.int32),
            pltpu.SemaphoreType.DMA((heads * 2 + 5,)),
            pltpu.SemaphoreType.DMA((heads * 24,)),
            pltpu.SemaphoreType.DMA((heads * 24,)),
        ]
    )
    smem = pl.BlockSpec(memory_space=pltpu.SMEM)
    vmem = pl.BlockSpec(memory_space=pltpu.VMEM)
    return pl.pallas_call(
        functools.partial(
            layer_kernel,
            heads=heads,
            quads=quads,
            tiles_here=tiles_here,
            block_len=block_len,
            model_width=model_width,
            span=span,
        ),
        in_specs=[smem, smem, vmem, vmem] + [pl.BlockSpec(memory_space=pl.ANY)] * 5,
        out_specs=vmem,
        out_shape=jax.ShapeDtypeStruct(cand_x.shape, b16),
        scratch_shapes=scratch,
        cost_estimate=pl.CostEstimate(
            flops=4 * tile_count * block_len * span * model_width,
            bytes_accessed=2 * history.size,
            transcendentals=tile_count * block_len * span * heads,
        ),
        compiler_params=pltpu.CompilerParams(
            collective_id=0, has_side_effects=True, vmem_limit_bytes=63 * 1024 * 1024
        ),
    )(user_row, hist_len, tile_user, pattern, cand_x, w_query, w_gate, w_out, history)


def per_device(cand_x, w_query, w_gate, w_out, history_kv, tile_user, user_row, hist_len, pattern):
    tiles_here, block_len, model_width = cand_x.shape
    own_rows, blocks_here, _, kv_width = history_kv.shape
    span = blocks_here * block_len
    history = history_kv.reshape(own_rows, span, kv_width)

    return layer(
        user_row, hist_len, tile_user[None, :], pattern.T, cand_x, w_query, w_gate, w_out, history
    )


def solution(mesh):
    return jax.shard_map(
        per_device,
        mesh=mesh,
        in_specs=(
            P(("cand", "hist"), None, None),
            P(),
            P(),
            P(),
            P("cand", "hist", None, None),
            P("cand"),
            P(),
            P(),
            P("cand", "hist"),
        ),
        out_specs=P(("cand", "hist"), None, None),
        check_vma=False,
    )
```

```python
import functools

import jax
import jax.numpy as jnp
from jax import lax
from jax.experimental import pallas as pl
from jax.experimental.pallas import tpu as pltpu
from jax.sharding import PartitionSpec as P

DH = 128
RING = 4
CORES = 2
QUAD = 4
MESH = pl.DeviceIdType.MESH
OWN_ROWS = 2
DIRECT_QUERIES = ()
DIRECT_SUMS = (7,)

norm_epsilon = 1e-05


STEPS = (
    ("kv_own", "kv_next", "kv_far", "q_own", "q_next", "q_line", "q_line_next")
    + ("compute0", "compute1", "compute2", "rs_one", "rs_two", "rs_three", "rs_four", "rs_five")
    + ("route", "gate_load", "gate")
)
ORDER = (
    24, 25, 1, 28, 29, 32, 33, 26, 27, 0, 30, 37, 40, 41, 8, 9,
    128, 38, 31, 36, 34, 120, 35, 136, 48, 3, 16, 2, 49, 42, 43, 44,
    56, 17, 64, 72, 11, 80, 57, 10, 50, 51, 65, 73, 88, 4, 18, 5,
    81, 45, 52, 58, 66, 89, 19, 12, 74, 96, 46, 7, 59, 82, 67, 13,
    53, 20, 75, 97, 6, 83, 90, 60, 15, 68, 76, 39, 105, 21, 104, 14,
    91, 47, 61, 112, 69, 22, 98, 84, 113, 77, 54, 55, 99, 23, 85, 106,
    92, 62, 70, 93, 107, 78, 114, 63, 71, 100, 86, 79, 115, 101, 87, 94,
    109, 108, 95, 116, 102, 117, 103, 110, 118, 119,
)


def layer_kernel(
    user_row_ref,
    hist_len_ref,
    tile_user_ref,
    pattern_ref,
    cand_ref,
    w_query_ref,
    w_gate_ref,
    w_out_ref,
    history_ref,
    mixed_ref,
    *scratch,
    heads,
    quads,
    tiles_here,
    block_len,
    model_width,
    span,
):
    scratch = list(scratch)

    def take(count):
        taken = scratch[:count]
        del scratch[:count]
        return taken

    kv = take(heads)
    q = take(heads)
    osort = take(1) + kv[: heads - 1]
    s1, s2p, s2m, r1a, r1b, r2m, r2p, keep = [take(2) for _ in range(8)]
    t1, t2p, t2m = [take(2) for _ in range(3)]
    u1, u2m, u2p = [take(2 + len(DIRECT_SUMS)) for _ in range(3)]
    x_in, weight, gate_act, mixing, squares, open_ref, table, table_smem = take(8)
    local_sem, send_sem, recv_sem = take(3)

    cand = lax.axis_index("cand")
    hist = lax.axis_index("hist")
    y, core = cand // CORES, cand % CORES
    z, x = hist // RING, hist % RING
    xp, xm, xo = (x + 1) % RING, (x + RING - 1) % RING, (x + 2) % RING
    zp, zm, zo = (z + 1) % RING, (z + RING - 1) % RING, (z + 2) % RING
    yp, ym, yo = [((y + d) % RING) * CORES + core for d in (1, RING - 1, 2)]
    dev_yp, dev_ym = (yp, hist), (ym, hist)
    dev_sib = (y * CORES + (CORES - 1 - core), hist)
    dev_xp, dev_xm = (cand, z * RING + xp), (cand, z * RING + xm)
    dev_zp, dev_zm = (cand, zp * RING + x), (cand, zm * RING + x)

    dev_xo, dev_zo = (cand, z * RING + xo), (cand, zo * RING + x)

    barrier = pltpu.get_barrier_semaphore()
    everyone = (dev_yp, dev_ym, dev_sib, dev_xp, dev_xm, dev_xo, dev_zp, dev_zm, dev_zo)
    for device in everyone:
        pl.semaphore_signal(barrier, inc=1, device_id=device, device_id_type=MESH)

    sends = {}
    per_head = 24

    def remote(src, dst, key, device):
        name, h = key
        number = h * per_head + KEYS.index(name)
        return pltpu.make_async_remote_copy(
            src_ref=src,
            dst_ref=dst,
            send_sem=send_sem.at[number],
            recv_sem=recv_sem.at[number],
            device_id=device,
            device_id_type=MESH,
        )

    def send(src, dst, name, h, device):
        copy = remote(src, dst, (name, h), device)
        copy.start()
        sends[(name, h)] = copy

    def arrive(dst, name, h):
        remote(dst, dst, (name, h), dev_sib).wait_recv()

    def sent(name, h):
        copy = sends.pop((name, h), None)
        if copy is not None:
            copy.wait_send()

    blocks = span // block_len
    row_size = 2 * blocks

    def own_copies(h):
        cols = pl.ds(h * DH, DH)
        value_cols = pl.ds((heads + h) * DH, DH)
        copies = []
        for r in range(OWN_ROWS):
            for k, columns in enumerate((cols, value_cols)):
                copies.append(
                    pltpu.make_async_copy(
                        history_ref.at[r, :, :, columns],
                        kv[h].at[pl.ds((cand * OWN_ROWS + r) * row_size + k * blocks, blocks)],
                        local_sem.at[(h * OWN_ROWS + r) * 2 + k],
                    )
                )
        return copies

    def fetch(src, dst, number):
        return pltpu.make_async_copy(src, dst, local_sem.at[2 * OWN_ROWS * heads + number])

    fetched = [
        fetch(cand_ref, x_in, 0),
        fetch(w_query_ref, weight, 1),
        fetch(w_gate_ref, weight, 2),
        fetch(table, table_smem, 3),
        fetch(w_out_ref, weight, 4),
    ]
    fetched[0].start()
    fetched[1].start()
    own = [own_copies(h) for h in range(heads)]
    for h in range(heads):
        for copy in own[h]:
            copy.start()
    fetched[0].wait()
    fetched[1].wait()

    def silu(v):
        return 0.5 * v + 0.5 * v * jnp.tanh(0.5 * v)

    def project(first, width):
        rows = x_in[...].reshape(tiles_here * block_len, model_width)
        product = jnp.dot(
            rows, weight[:, first : first + width], preferred_element_type=jnp.float32
        )
        return silu(product).astype(jnp.bfloat16)

    def project_pair(h):
        both = project(h * DH, 2 * DH)
        for n in range(2):
            mine = both[:, n * DH : (n + 1) * DH].reshape(tiles_here, block_len, DH)
            q[h + n][z, pl.ds(x * tiles_here, tiles_here)] = mine

    project_pair(0)
    pl.semaphore_wait(barrier, len(everyone))

    def gate_load(h):
        fetched[2].start()

    def gate(h):
        fetched[2].wait()
        width = 2 * DH
        for first in range(0, model_width, width):
            gate_act[:, first : first + width] = project(first, width)
        fetched[4].start()

    def route(h):
        tile_count = tile_user_ref.shape[1]
        i32 = jnp.int32
        tile_user = tile_user_ref[...]
        rows = jnp.zeros_like(tile_user)
        lengths = jnp.zeros_like(tile_user)
        for user in range(user_row_ref.shape[0]):
            hit = tile_user == user
            rows = jnp.where(hit, user_row_ref[user], rows)
            lengths = jnp.where(hit, hist_len_ref[user], lengths)
        square = (tile_count, tile_count)
        down, along = lax.broadcasted_iota(i32, square, 0), lax.broadcasted_iota(i32, square, 1)

        def column(v):
            return jnp.sum(
                jnp.where(down == along, jnp.broadcast_to(v, square), 0), axis=1, keepdims=True
            )

        rank = jnp.sum(
            jnp.where((column(rows) == rows) & (down < along), 1, 0), axis=0, keepdims=True
        )
        row_ids = lax.broadcasted_iota(i32, (user_row_ref.shape[0], tile_count), 0)
        count = jnp.sum(jnp.where(row_ids == rows, 1, 0), axis=1, keepdims=True)
        need = lax.shift_right_logical(count + (QUAD - 1), jnp.full_like(count, 2))
        first = jnp.sum(jnp.where(row_ids < rows, need, 0), axis=0, keepdims=True)
        tile_slot = QUAD * first + rank
        wide = (tile_count, table.shape[1])
        slot_tile = jnp.sum(
            jnp.where(
                column(tile_slot) == lax.broadcasted_iota(i32, wide, 1),
                lax.broadcasted_iota(i32, wide, 0),
                0,
            ),
            axis=0,
            keepdims=True,
        )
        table[...] = jnp.zeros_like(table)
        table[0:1, :] = slot_tile
        table[1:2, 0:tile_count] = tile_slot
        table[2:3, 0:tile_count] = rows
        fetched[3].start()
        positions = hist * span + lax.broadcasted_iota(i32, (tile_count, span), 1)
        pattern = pattern_ref[...]
        block_open = jnp.concatenate(
            [
                jnp.broadcast_to(column(pattern[b : b + 1, :]), (tile_count, block_len))
                for b in range(pattern.shape[0])
            ],
            axis=1,
        )
        length = jnp.broadcast_to(column(lengths), (tile_count, span))
        allowed = (positions < length) & (block_open > 0)
        open_ref[...] = jnp.where(allowed, 1.0 / length.astype(jnp.float32), 0.0)
        fetched[3].wait()

    def pair_of(owner):
        return pl.ds(owner * OWN_ROWS * row_size, OWN_ROWS * row_size)

    def one_of(owner, r):
        return pl.ds((owner * OWN_ROWS + r) * row_size, row_size)

    other = 1 - 2 * core

    def kv_own(h):
        for copy in own[h]:
            copy.wait()
        mine = kv[h].at[pair_of(cand)]
        send(mine, mine, "kv+", h, dev_yp)
        send(mine, mine, "kv-", h, dev_ym)
        send(mine, mine, "kvs0", h, dev_sib)

    def kv_next(h):
        below, above = kv[h].at[pair_of(ym)], kv[h].at[pair_of(yp)]
        arrive(below, "kv+", h)
        first = kv[h].at[one_of(ym, 0)]
        send(first, first, "kvf+", h, dev_yp)
        send(below, below, "kvs1", h, dev_sib)
        arrive(above, "kv-", h)
        second = kv[h].at[one_of(yp, 1)]
        send(second, second, "kvf-", h, dev_ym)
        send(above, above, "kvs2", h, dev_sib)

    def kv_far(h):
        arrive(kv[h].at[one_of(yo, 0)], "kvf+", h)
        arrive(kv[h].at[one_of(yo, 1)], "kvf-", h)
        far = kv[h].at[pair_of(yo)]
        send(far, far, "kvs3", h, dev_sib)

    def kv_ready(h):
        for number, owner in enumerate((cand, ym, yp, yo)):
            arrive(kv[h].at[pair_of(owner + other)], "kvs%d" % number, h)

    def slot(h, zz, xx, start=0, size=tiles_here):
        return q[h].at[zz, pl.ds(xx * tiles_here + start, size)]

    half = tiles_here // 2

    def q_own(h):
        if h % 2 == 0 and h > 0:
            project_pair(h)
        mine = slot(h, z, x)
        first = h % 2 == 0
        send(mine, mine, "q+", h, dev_xp if first else dev_zp)
        send(mine, mine, "q-", h, dev_xm if first else dev_zm)
        if h in DIRECT_QUERIES:
            send(mine, mine, "qf+", h, dev_xo if first else dev_zo)

    def q_next(h):
        if h % 2 == 0:
            low, high, dp, dm = (z, xm), (z, xp), dev_xp, dev_xm
        else:
            low, high, dp, dm = (zm, x), (zp, x), dev_zp, dev_zm
        arrive(slot(h, *low), "q+", h)
        part = slot(h, *low, 0, half)
        send(part, part, "qf+", h, dp)
        arrive(slot(h, *high), "q-", h)
        part = slot(h, *high, half, half)
        send(part, part, "qf-", h, dm)

    def line(h, at, part=None):
        if h % 2 == 0:
            width = RING * tiles_here
            begin, size = {None: (0, width), 0: (0, width // 2), 1: (width // 2, width // 2)}[part]
            return q[h].at[at, pl.ds(begin, size)]
        begin, size = {None: (0, RING), 0: (0, RING // 2), 1: (RING // 2, RING // 2)}[part]
        return q[h].at[pl.ds(begin, size), pl.ds(at * tiles_here, tiles_here)]

    def q_line(h):
        first = h % 2 == 0
        far = (z, xo) if first else (zo, x)
        if h in DIRECT_QUERIES:
            arrive(slot(h, *((z, xm) if first else (zm, x))), "q+", h)
            arrive(slot(h, *((z, xp) if first else (zp, x))), "q-", h)
            arrive(slot(h, *far), "qf+", h)
        else:
            arrive(slot(h, *far, 0, half), "qf+", h)
            arrive(slot(h, *far, half, half), "qf-", h)
        at, dp, dm = (z, dev_zp, dev_zm) if h % 2 == 0 else (x, dev_xp, dev_xm)
        mine = line(h, at)
        send(mine, mine, "l+", h, dp)
        send(mine, mine, "l-", h, dm)

    def q_line_next(h):
        low, high, dp, dm = (zm, zp, dev_zp, dev_zm) if h % 2 == 0 else (xm, xp, dev_xp, dev_xm)
        arrive(line(h, low), "l+", h)
        part = line(h, low, 0)
        send(part, part, "lf+", h, dp)
        arrive(line(h, high), "l-", h)
        part = line(h, high, 1)
        send(part, part, "lf-", h, dm)

    def q_ready(h):
        far = zo if h % 2 == 0 else xo
        arrive(line(h, far, 0), "lf+", h)
        arrive(line(h, far, 1), "lf-", h)

    half_scale = 0.5 / DH**0.5

    def quad(h, number):
        tiles = [table_smem[0, number * QUAD + a] for a in range(QUAD)]
        row = table_smem[2, tiles[0]]
        group = RING * tiles_here
        block = jnp.concatenate([q[h][t // group, t % group] for t in tiles], axis=0)
        scores = lax.dot_general(
            block,
            kv[h][pl.ds(row * row_size, blocks)].reshape(span, DH),
            (((1,), (1,)), ((), ())),
            preferred_element_type=jnp.float32,
        )
        weights = []
        for a in range(QUAD):
            part = (scores[a * DH : (a + 1) * DH] * half_scale).astype(jnp.bfloat16)
            weights.append((part + part * jnp.tanh(part)) * open_ref[pl.ds(tiles[a], 1), :].astype(jnp.bfloat16))
        out = jnp.dot(
            jnp.concatenate(weights, axis=0),
            kv[h][pl.ds(row * row_size + blocks, blocks)].reshape(span, DH),
            preferred_element_type=jnp.float32,
        ).astype(jnp.bfloat16)
        for a in range(QUAD):
            osort[h][number * QUAD + a] = out[a * DH : (a + 1) * DH]

    third = (quads + 2) // 3
    cuts = (0, third, 2 * third, quads)
    unroll = 4

    def compute(part, h):
        if part == 0:
            kv_ready(h)
            q_ready(h)
            for name in KEYS[:8]:
                sent(name, h - 1)
        first, last = cuts[part], cuts[part + 1]
        whole = (last - first) // unroll

        def body(i, carry):
            for j in range(unroll):
                quad(h, first + i * unroll + j)
            return carry

        lax.fori_loop(0, whole, body, 0)
        for number in range(first + whole * unroll, last):
            quad(h, number)

    def tile_at(h, at, j, i):
        return ((j * RING + at) if h % 2 == 0 else (at * RING + j)) * tiles_here + i

    def partial(h, at, j, i):
        return osort[h][table_smem[1, tile_at(h, at, j, i)]]

    def each_tile(body, first=0, last=RING):
        def step(n, carry):
            for i in range(tiles_here):
                body(n, i)
            return carry

        lax.fori_loop(first, last, step, 0)

    f32 = jnp.float32
    b16 = jnp.bfloat16

    def axis_one(h):
        return (x, xp, xm, xo, dev_xp, dev_xm) if h % 2 == 0 else (z, zp, zm, zo, dev_zp, dev_zm)

    def axis_two(h):
        return axis_one(h + 1)

    def rs_one(h):
        e = h % 2
        at, up, down, far, dp, dm = axis_one(h)
        for name in ("a+", "a-"):
            sent(name, h - 2)

        def body(j, i):
            s1[e][j, i] = partial(h, far, j, i)

        each_tile(body)
        send(s1[e].at[pl.ds(0, 2)], r1a[e], "a+", h, dp)
        send(s1[e].at[pl.ds(2, 2)], r1b[e], "a-", h, dm)

    def rs_two(h):
        e = h % 2
        at, up, down, far, dp, dm = axis_one(h)
        arrive(r1a[e], "a+", h)
        arrive(r1b[e], "a-", h)
        for name in ("b+", "b-"):
            sent(name, h - 2)

        def low(j, i):
            s2p[e][j, i] = (partial(h, up, j, i).astype(f32) + r1a[e][j, i].astype(f32)).astype(b16)
            s2m[e][j, i] = partial(h, down, j, i)

        def high(j, i):
            s2p[e][j, i] = partial(h, up, j, i)
            s2m[e][j, i] = (
                partial(h, down, j, i).astype(f32) + r1b[e][j - 2, i].astype(f32)
            ).astype(b16)

        each_tile(low, 0, 2)
        each_tile(high, 2, 4)
        send(s2p[e], r2m[e], "b+", h, dp)
        send(s2m[e], r2p[e], "b-", h, dm)

    def landing(h):
        return 2 + DIRECT_SUMS.index(h) if h in DIRECT_SUMS else h % 2

    def rs_three(h):
        e = h % 2
        u = landing(h)
        at = axis_one(h)[0]
        _, up, down, far, dp, dm = axis_two(h)
        arrive(r2m[e], "b+", h)
        arrive(r2p[e], "b-", h)
        for name in ("c+", "c-"):
            sent(name, h - 2)

        def body(j, i):
            keep[e][j, i] = (
                partial(h, at, j, i).astype(f32)
                + r2m[e][j, i].astype(f32)
                + r2p[e][j, i].astype(f32)
            ).astype(keep[e].dtype)

        each_tile(body)
        for i in range(tiles_here):
            t1[e][i] = keep[e][far, i].astype(b16)
        if h not in DIRECT_SUMS:
            send(t1[e].at[pl.ds(0, half)], u1[u].at[pl.ds(0, half)], "c+", h, dp)
            send(t1[e].at[pl.ds(half, half)], u1[u].at[pl.ds(half, half)], "c-", h, dm)
            return
        for name in ("d+", "d-"):
            sent(name, h - 2)
        for i in range(tiles_here):
            t2p[e][i] = keep[e][up, i].astype(b16)
            t2m[e][i] = keep[e][down, i].astype(b16)
        send(t2p[e], u2m[u], "d+", h, dp)
        send(t2m[e], u2p[u], "d-", h, dm)
        send(t1[e], u1[u], "c+", h, dev_zo if h % 2 == 0 else dev_xo)

    def rs_four(h):
        e = h % 2
        u = landing(h)
        _, up, down, _, dp, dm = axis_two(h)
        arrive(u1[u].at[pl.ds(0, half)], "c+", h)
        arrive(u1[u].at[pl.ds(half, half)], "c-", h)
        for name in ("d+", "d-"):
            sent(name, h - 2)
        for i in range(tiles_here):
            to_up, to_down = keep[e][up, i].astype(f32), keep[e][down, i].astype(f32)
            if i < half:
                to_up = to_up + u1[u][i].astype(f32)
            else:
                to_down = to_down + u1[u][i].astype(f32)
            t2p[e][i] = to_up.astype(b16)
            t2m[e][i] = to_down.astype(b16)
        send(t2p[e], u2m[u], "d+", h, dp)
        send(t2m[e], u2p[u], "d-", h, dm)

    def rs_five(h):
        e = h % 2
        u = landing(h)
        at = axis_two(h)[0]
        arrive(u2m[u], "d+", h)
        arrive(u2p[u], "d-", h)
        direct = h in DIRECT_SUMS
        if direct:
            arrive(u1[u], "c+", h)
        cols = slice(h * DH, (h + 1) * DH)
        total = keep[e][at].astype(f32) + u2m[u][...].astype(f32) + u2p[u][...].astype(f32)
        if direct:
            total = total + u1[u][...].astype(f32)
        total = total.reshape(tiles_here * block_len, DH)
        hidden = (total * gate_act[:, cols].astype(f32)).astype(b16)
        if not mixed_heads:
            fetched[4].wait()
        for first in range(0, model_width, 2 * DH):
            wide = slice(first, first + 2 * DH)
            product = jnp.dot(hidden, weight[cols, wide], preferred_element_type=f32)
            mixing[:, wide] = mixing[:, wide] + product if mixed_heads else product
        squares[...] = squares[...] + total * total if mixed_heads else total * total
        mixed_heads.append(h)

    mixed_heads = []

    def finish():
        mean_square = jnp.sum(squares[...], axis=1, keepdims=True) * (1.0 / model_width)
        scale = lax.rsqrt(mean_square + norm_epsilon)
        for i in range(tiles_here):
            rows = slice(i * block_len, (i + 1) * block_len)
            mixed_ref[i] = (mixing[rows, :] * scale[rows] + x_in[i].astype(f32)).astype(b16)

    run = {
        "kv_own": kv_own,
        "kv_next": kv_next,
        "kv_far": kv_far,
        "q_own": q_own,
        "q_next": q_next,
        "q_line": q_line,
        "q_line_next": q_line_next,
        "compute0": functools.partial(compute, 0),
        "compute1": functools.partial(compute, 1),
        "compute2": functools.partial(compute, 2),
        "rs_one": rs_one,
        "rs_two": rs_two,
        "rs_three": rs_three,
        "rs_four": rs_four,
        "rs_five": rs_five,
        "route": route,
        "gate_load": gate_load,
        "gate": gate,
    }
    for code in ORDER:
        run[STEPS[code // 8]](code % 8)
    finish()
    for name, h in list(sends):
        sent(name, h)


KEYS = (
    ("kv+", "kv-", "kvf+", "kvf-", "kvs0", "kvs1", "kvs2", "kvs3")
    + ("q+", "q-", "qf+", "qf-", "l+", "l-", "lf+", "lf-")
    + ("a+", "a-", "b+", "b-", "c+", "c-", "d+", "d-")
)


def layer(user_row, hist_len, tile_user, pattern, cand_x, w_query, w_gate, w_out, history):
    tiles_here, block_len, model_width = cand_x.shape
    heads = model_width // DH
    tile_count = tile_user.shape[1]
    cache_rows = CORES * RING * OWN_ROWS
    quads = (tile_count + (QUAD - 1) * cache_rows // 2) // QUAD
    blocks = history.shape[1]
    span = blocks * block_len
    b16 = jnp.bfloat16
    tile = (block_len, DH)
    lines = pltpu.VMEM((RING, tiles_here) + tile, b16)
    half_lines = pltpu.VMEM((RING // 2, tiles_here) + tile, b16)
    few = pltpu.VMEM((tiles_here,) + tile, b16)
    scratch = (
        [pltpu.VMEM((cache_rows * 2 * blocks,) + tile, b16)] * heads
        + [pltpu.VMEM((RING, RING * tiles_here) + tile, b16)] * heads
        + [pltpu.VMEM((quads * QUAD,) + tile, b16)]
        + [lines] * 2
        + [lines] * 4
        + [half_lines] * 4
        + [lines] * 4
        + [lines] * 2
        + [few] * 6
        + [few] * (6 + 3 * len(DIRECT_SUMS))
        + [
            pltpu.VMEM(cand_x.shape, b16),
            pltpu.VMEM(w_query.shape, b16),
            pltpu.VMEM((tiles_here * block_len, model_width), b16),
            pltpu.VMEM((tiles_here * block_len, model_width), jnp.float32),
            pltpu.VMEM((tiles_here * block_len, DH), jnp.float32),
            pltpu.VMEM((tile_count, span), jnp.float32),
            pltpu.VMEM((8, DH), jnp.int32),
            pltpu.SMEM((8, DH), jnp.int32),
            pltpu.SemaphoreType.DMA((heads * OWN_ROWS * 2 + 5,)),
            pltpu.SemaphoreType.DMA((heads * 24,)),
            pltpu.SemaphoreType.DMA((heads * 24,)),
        ]
    )
    smem = pl.BlockSpec(memory_space=pltpu.SMEM)
    vmem = pl.BlockSpec(memory_space=pltpu.VMEM)
    return pl.pallas_call(
        functools.partial(
            layer_kernel,
            heads=heads,
            quads=quads,
            tiles_here=tiles_here,
            block_len=block_len,
            model_width=model_width,
            span=span,
        ),
        in_specs=[smem, smem, vmem, vmem] + [pl.BlockSpec(memory_space=pl.ANY)] * 5,
        out_specs=vmem,
        out_shape=jax.ShapeDtypeStruct(cand_x.shape, b16),
        scratch_shapes=scratch,
        cost_estimate=pl.CostEstimate(
            flops=4 * tile_count * block_len * span * model_width,
            bytes_accessed=2 * history.size,
            transcendentals=tile_count * block_len * span * heads,
        ),
        compiler_params=pltpu.CompilerParams(
            collective_id=0, has_side_effects=True, vmem_limit_bytes=63 * 1024 * 1024
        ),
    )(user_row, hist_len, tile_user, pattern, cand_x, w_query, w_gate, w_out, history)


def per_device(cand_x, w_query, w_gate, w_out, history_kv, tile_user, user_row, hist_len, pattern):
    return layer(
        user_row, hist_len, tile_user[None, :], pattern.T, cand_x, w_query, w_gate, w_out, history_kv
    )


def solution(mesh):
    return jax.shard_map(
        per_device,
        mesh=mesh,
        in_specs=(
            P(("cand", "hist"), None, None),
            P(),
            P(),
            P(),
            P("cand", "hist", None, None),
            P("cand"),
            P(),
            P(),
            P("cand", "hist"),
        ),
        out_specs=P(("cand", "hist"), None, None),
        check_vma=False,
    )
```

```python
import functools

import jax
import jax.numpy as jnp
from jax import lax
from jax.experimental import pallas as pl
from jax.experimental.pallas import tpu as pltpu
from jax.sharding import PartitionSpec as P

DH = 128
RING = 4
CORES = 2
QUAD = 4
MESH = pl.DeviceIdType.MESH
OWN_ROWS = 2
DIRECT_QUERIES = ()
DIRECT_SUMS = (7,)

norm_epsilon = 1e-05


STEPS = (
    ("kv_own", "kv_next", "kv_far", "q_own", "q_next", "q_line", "q_line_next")
    + ("compute0", "compute1", "compute2", "rs_one", "rs_two", "rs_three", "rs_four", "rs_five")
    + ("route", "gate_load", "gate")
)
ORDER = (
    24, 25, 0, 1, 26, 27, 32, 33, 28, 29, 30, 34, 35, 128, 40, 31,
    8, 41, 2, 9, 136, 36, 37, 43, 120, 48, 16, 42, 49, 10, 44, 3,
    4, 56, 17, 5, 64, 72, 38, 80, 57, 65, 51, 50, 18, 73, 88, 81,
    52, 45, 12, 11, 39, 6, 58, 66, 89, 74, 19, 96, 13, 82, 46, 20,
    59, 7, 67, 53, 75, 14, 97, 90, 83, 60, 21, 104, 68, 105, 47, 15,
    54, 76, 91, 22, 61, 112, 69, 98, 84, 77, 23, 62, 55, 113, 99, 85,
    92, 70, 106, 78, 93, 63, 71, 107, 114, 100, 86, 79, 115, 101, 87, 108,
    94, 109, 95, 116, 102, 117, 103, 110, 118, 119,
)


def layer_kernel(
    user_row_ref,
    hist_len_ref,
    tile_user_ref,
    pattern_ref,
    cand_ref,
    w_query_ref,
    w_gate_ref,
    w_out_ref,
    history_ref,
    mixed_ref,
    *scratch,
    heads,
    quads,
    tiles_here,
    block_len,
    model_width,
    span,
):
    scratch = list(scratch)

    def take(count):
        taken = scratch[:count]
        del scratch[:count]
        return taken

    kv = take(heads)
    q = take(heads)
    osort = take(1) + kv[: heads - 1]
    s1, s2p, s2m, r1a, r1b, r2m, r2p, keep = [take(2) for _ in range(8)]
    t1, t2p, t2m = [take(2) for _ in range(3)]
    u1, u2m, u2p = [take(2 + len(DIRECT_SUMS)) for _ in range(3)]
    x_in, weight, gate_act, mixing, squares, open_ref, table, table_smem = take(8)
    local_sem, send_sem, recv_sem = take(3)

    cand = lax.axis_index("cand")
    hist = lax.axis_index("hist")
    y, core = cand // CORES, cand % CORES
    z, x = hist // RING, hist % RING
    xp, xm, xo = (x + 1) % RING, (x + RING - 1) % RING, (x + 2) % RING
    zp, zm, zo = (z + 1) % RING, (z + RING - 1) % RING, (z + 2) % RING
    yp, ym, yo = [((y + d) % RING) * CORES + core for d in (1, RING - 1, 2)]
    dev_yp, dev_ym = (yp, hist), (ym, hist)
    dev_sib = (y * CORES + (CORES - 1 - core), hist)
    dev_xp, dev_xm = (cand, z * RING + xp), (cand, z * RING + xm)
    dev_zp, dev_zm = (cand, zp * RING + x), (cand, zm * RING + x)

    dev_xo, dev_zo = (cand, z * RING + xo), (cand, zo * RING + x)

    barrier = pltpu.get_barrier_semaphore()
    everyone = (dev_yp, dev_ym, dev_sib, dev_xp, dev_xm, dev_xo, dev_zp, dev_zm, dev_zo)
    for device in everyone:
        pl.semaphore_signal(barrier, inc=1, device_id=device, device_id_type=MESH)

    sends = {}
    per_head = 24

    def remote(src, dst, key, device):
        name, h = key
        number = h * per_head + KEYS.index(name)
        return pltpu.make_async_remote_copy(
            src_ref=src,
            dst_ref=dst,
            send_sem=send_sem.at[number],
            recv_sem=recv_sem.at[number],
            device_id=device,
            device_id_type=MESH,
        )

    def send(src, dst, name, h, device):
        copy = remote(src, dst, (name, h), device)
        copy.start()
        sends[(name, h)] = copy

    def arrive(dst, name, h):
        remote(dst, dst, (name, h), dev_sib).wait_recv()

    def sent(name, h):
        copy = sends.pop((name, h), None)
        if copy is not None:
            copy.wait_send()

    blocks = span // block_len
    row_size = 2 * blocks

    def own_copies(h):
        cols = pl.ds(h * DH, DH)
        value_cols = pl.ds((heads + h) * DH, DH)
        copies = []
        for r in range(OWN_ROWS):
            for k, columns in enumerate((cols, value_cols)):
                copies.append(
                    pltpu.make_async_copy(
                        history_ref.at[r, :, :, columns],
                        kv[h].at[pl.ds((cand * OWN_ROWS + r) * row_size + k * blocks, blocks)],
                        local_sem.at[(h * OWN_ROWS + r) * 2 + k],
                    )
                )
        return copies

    def fetch(src, dst, number):
        return pltpu.make_async_copy(src, dst, local_sem.at[2 * OWN_ROWS * heads + number])

    fetched = [
        fetch(cand_ref, x_in, 0),
        fetch(w_query_ref.at[:, pl.ds(0, 2 * DH)], weight.at[:, pl.ds(0, 2 * DH)], 1),
        fetch(w_gate_ref, weight, 2),
        fetch(table, table_smem, 3),
        fetch(w_out_ref, weight, 4),
        fetch(
            w_query_ref.at[:, pl.ds(2 * DH, model_width - 2 * DH)],
            weight.at[:, pl.ds(2 * DH, model_width - 2 * DH)],
            5,
        ),
    ]
    fetched[0].start()
    fetched[1].start()
    fetched[5].start()
    own = [own_copies(h) for h in range(heads)]
    for h in range(heads):
        for copy in own[h]:
            copy.start()
    fetched[0].wait()
    fetched[1].wait()

    def silu(v):
        return 0.5 * v + 0.5 * v * jnp.tanh(0.5 * v)

    def project(first, width):
        rows = x_in[...].reshape(tiles_here * block_len, model_width)
        product = jnp.dot(
            rows, weight[:, first : first + width], preferred_element_type=jnp.float32
        )
        return silu(product).astype(jnp.bfloat16)

    def project_pair(h):
        both = project(h * DH, 2 * DH)
        for n in range(2):
            mine = both[:, n * DH : (n + 1) * DH].reshape(tiles_here, block_len, DH)
            q[h + n][z, pl.ds(x * tiles_here, tiles_here)] = mine

    project_pair(0)
    pl.semaphore_wait(barrier, len(everyone))
    later_columns = [fetched[5]]

    def gate_load(h):
        fetched[2].start()

    def gate(h):
        fetched[2].wait()
        width = 2 * DH
        for first in range(0, model_width, width):
            gate_act[:, first : first + width] = project(first, width)
        fetched[4].start()

    def route(h):
        tile_count = tile_user_ref.shape[1]
        i32 = jnp.int32
        tile_user = tile_user_ref[...]
        rows = jnp.zeros_like(tile_user)
        lengths = jnp.zeros_like(tile_user)
        for user in range(user_row_ref.shape[0]):
            hit = tile_user == user
            rows = jnp.where(hit, user_row_ref[user], rows)
            lengths = jnp.where(hit, hist_len_ref[user], lengths)
        square = (tile_count, tile_count)
        down, along = lax.broadcasted_iota(i32, square, 0), lax.broadcasted_iota(i32, square, 1)

        def column(v):
            return jnp.sum(
                jnp.where(down == along, jnp.broadcast_to(v, square), 0), axis=1, keepdims=True
            )

        rank = jnp.sum(
            jnp.where((column(rows) == rows) & (down < along), 1, 0), axis=0, keepdims=True
        )
        row_ids = lax.broadcasted_iota(i32, (user_row_ref.shape[0], tile_count), 0)
        count = jnp.sum(jnp.where(row_ids == rows, 1, 0), axis=1, keepdims=True)
        need = lax.shift_right_logical(count + (QUAD - 1), jnp.full_like(count, 2))
        first = jnp.sum(jnp.where(row_ids < rows, need, 0), axis=0, keepdims=True)
        tile_slot = QUAD * first + rank
        wide = (tile_count, table.shape[1])
        slot_tile = jnp.sum(
            jnp.where(
                column(tile_slot) == lax.broadcasted_iota(i32, wide, 1),
                lax.broadcasted_iota(i32, wide, 0),
                0,
            ),
            axis=0,
            keepdims=True,
        )
        table[...] = jnp.zeros_like(table)
        table[0:1, :] = slot_tile
        table[1:2, 0:tile_count] = tile_slot
        table[2:3, 0:tile_count] = rows
        fetched[3].start()
        positions = hist * span + lax.broadcasted_iota(i32, (tile_count, span), 1)
        pattern = pattern_ref[...]
        block_open = jnp.concatenate(
            [
                jnp.broadcast_to(column(pattern[b : b + 1, :]), (tile_count, block_len))
                for b in range(pattern.shape[0])
            ],
            axis=1,
        )
        length = jnp.broadcast_to(column(lengths), (tile_count, span))
        allowed = (positions < length) & (block_open > 0)
        open_ref[...] = jnp.where(allowed, 1.0 / length.astype(jnp.float32), 0.0)
        fetched[3].wait()

    def pair_of(owner):
        return pl.ds(owner * OWN_ROWS * row_size, OWN_ROWS * row_size)

    def one_of(owner, r):
        return pl.ds((owner * OWN_ROWS + r) * row_size, row_size)

    other = 1 - 2 * core

    def kv_own(h):
        for copy in own[h]:
            copy.wait()
        mine = kv[h].at[pair_of(cand)]
        send(mine, mine, "kv+", h, dev_yp)
        send(mine, mine, "kv-", h, dev_ym)
        send(mine, mine, "kvs0", h, dev_sib)

    def kv_next(h):
        below, above = kv[h].at[pair_of(ym)], kv[h].at[pair_of(yp)]
        arrive(below, "kv+", h)
        first = kv[h].at[one_of(ym, 0)]
        send(first, first, "kvf+", h, dev_yp)
        send(below, below, "kvs1", h, dev_sib)
        arrive(above, "kv-", h)
        second = kv[h].at[one_of(yp, 1)]
        send(second, second, "kvf-", h, dev_ym)
        send(above, above, "kvs2", h, dev_sib)

    def kv_far(h):
        arrive(kv[h].at[one_of(yo, 0)], "kvf+", h)
        arrive(kv[h].at[one_of(yo, 1)], "kvf-", h)
        far = kv[h].at[pair_of(yo)]
        send(far, far, "kvs3", h, dev_sib)

    def kv_ready(h):
        for number, owner in enumerate((cand, ym, yp, yo)):
            arrive(kv[h].at[pair_of(owner + other)], "kvs%d" % number, h)

    def slot(h, zz, xx, start=0, size=tiles_here):
        return q[h].at[zz, pl.ds(xx * tiles_here + start, size)]

    half = tiles_here // 2

    def q_own(h):
        if h % 2 == 0 and h > 0:
            while later_columns:
                later_columns.pop().wait()
            project_pair(h)
        mine = slot(h, z, x)
        first = h % 2 == 0
        send(mine, mine, "q+", h, dev_xp if first else dev_zp)
        send(mine, mine, "q-", h, dev_xm if first else dev_zm)
        if h in DIRECT_QUERIES:
            send(mine, mine, "qf+", h, dev_xo if first else dev_zo)

    def q_next(h):
        if h % 2 == 0:
            low, high, dp, dm = (z, xm), (z, xp), dev_xp, dev_xm
        else:
            low, high, dp, dm = (zm, x), (zp, x), dev_zp, dev_zm
        arrive(slot(h, *low), "q+", h)
        part = slot(h, *low, 0, half)
        send(part, part, "qf+", h, dp)
        arrive(slot(h, *high), "q-", h)
        part = slot(h, *high, half, half)
        send(part, part, "qf-", h, dm)

    def line(h, at, part=None):
        if h % 2 == 0:
            width = RING * tiles_here
            begin, size = {None: (0, width), 0: (0, width // 2), 1: (width // 2, width // 2)}[part]
            return q[h].at[at, pl.ds(begin, size)]
        begin, size = {None: (0, RING), 0: (0, RING // 2), 1: (RING // 2, RING // 2)}[part]
        return q[h].at[pl.ds(begin, size), pl.ds(at * tiles_here, tiles_here)]

    def q_line(h):
        first = h % 2 == 0
        far = (z, xo) if first else (zo, x)
        if h in DIRECT_QUERIES:
            arrive(slot(h, *((z, xm) if first else (zm, x))), "q+", h)
            arrive(slot(h, *((z, xp) if first else (zp, x))), "q-", h)
            arrive(slot(h, *far), "qf+", h)
        else:
            arrive(slot(h, *far, 0, half), "qf+", h)
            arrive(slot(h, *far, half, half), "qf-", h)
        at, dp, dm = (z, dev_zp, dev_zm) if h % 2 == 0 else (x, dev_xp, dev_xm)
        mine = line(h, at)
        send(mine, mine, "l+", h, dp)
        send(mine, mine, "l-", h, dm)

    def q_line_next(h):
        low, high, dp, dm = (zm, zp, dev_zp, dev_zm) if h % 2 == 0 else (xm, xp, dev_xp, dev_xm)
        arrive(line(h, low), "l+", h)
        part = line(h, low, 0)
        send(part, part, "lf+", h, dp)
        arrive(line(h, high), "l-", h)
        part = line(h, high, 1)
        send(part, part, "lf-", h, dm)

    def q_ready(h):
        far = zo if h % 2 == 0 else xo
        arrive(line(h, far, 0), "lf+", h)
        arrive(line(h, far, 1), "lf-", h)

    half_scale = 0.5 / DH**0.5

    def quad(h, number):
        tiles = [table_smem[0, number * QUAD + a] for a in range(QUAD)]
        row = table_smem[2, tiles[0]]
        group = RING * tiles_here
        block = jnp.concatenate([q[h][t // group, t % group] for t in tiles], axis=0)
        scores = lax.dot_general(
            block,
            kv[h][pl.ds(row * row_size, blocks)].reshape(span, DH),
            (((1,), (1,)), ((), ())),
            preferred_element_type=jnp.float32,
        )
        weights = []
        for a in range(QUAD):
            part = (scores[a * DH : (a + 1) * DH] * half_scale).astype(jnp.bfloat16)
            weights.append((part + part * jnp.tanh(part)) * open_ref[pl.ds(tiles[a], 1), :].astype(jnp.bfloat16))
        out = jnp.dot(
            jnp.concatenate(weights, axis=0),
            kv[h][pl.ds(row * row_size + blocks, blocks)].reshape(span, DH),
            preferred_element_type=jnp.float32,
        ).astype(jnp.bfloat16)
        for a in range(QUAD):
            osort[h][number * QUAD + a] = out[a * DH : (a + 1) * DH]

    third = (quads + 2) // 3
    cuts = (0, third, 2 * third, quads)
    unroll = 4

    def compute(part, h):
        if part == 0:
            kv_ready(h)
            q_ready(h)
            for name in KEYS[:8]:
                sent(name, h - 1)
        first, last = cuts[part], cuts[part + 1]
        whole = (last - first) // unroll

        def body(i, carry):
            for j in range(unroll):
                quad(h, first + i * unroll + j)
            return carry

        lax.fori_loop(0, whole, body, 0)
        for number in range(first + whole * unroll, last):
            quad(h, number)

    def tile_at(h, at, j, i):
        return ((j * RING + at) if h % 2 == 0 else (at * RING + j)) * tiles_here + i

    def partial(h, at, j, i):
        return osort[h][table_smem[1, tile_at(h, at, j, i)]]

    def each_tile(body, first=0, last=RING):
        def step(n, carry):
            for i in range(tiles_here):
                body(n, i)
            return carry

        lax.fori_loop(first, last, step, 0)

    f32 = jnp.float32
    b16 = jnp.bfloat16

    def axis_one(h):
        return (x, xp, xm, xo, dev_xp, dev_xm) if h % 2 == 0 else (z, zp, zm, zo, dev_zp, dev_zm)

    def axis_two(h):
        return axis_one(h + 1)

    def rs_one(h):
        e = h % 2
        at, up, down, far, dp, dm = axis_one(h)
        for name in ("a+", "a-"):
            sent(name, h - 2)

        def body(j, i):
            s1[e][j, i] = partial(h, far, j, i)

        each_tile(body)
        send(s1[e].at[pl.ds(0, 2)], r1a[e], "a+", h, dp)
        send(s1[e].at[pl.ds(2, 2)], r1b[e], "a-", h, dm)

    def rs_two(h):
        e = h % 2
        at, up, down, far, dp, dm = axis_one(h)
        arrive(r1a[e], "a+", h)
        arrive(r1b[e], "a-", h)
        for name in ("b+", "b-"):
            sent(name, h - 2)

        def low(j, i):
            s2p[e][j, i] = (partial(h, up, j, i).astype(f32) + r1a[e][j, i].astype(f32)).astype(b16)
            s2m[e][j, i] = partial(h, down, j, i)

        def high(j, i):
            s2p[e][j, i] = partial(h, up, j, i)
            s2m[e][j, i] = (
                partial(h, down, j, i).astype(f32) + r1b[e][j - 2, i].astype(f32)
            ).astype(b16)

        each_tile(low, 0, 2)
        each_tile(high, 2, 4)
        send(s2p[e], r2m[e], "b+", h, dp)
        send(s2m[e], r2p[e], "b-", h, dm)

    def landing(h):
        return 2 + DIRECT_SUMS.index(h) if h in DIRECT_SUMS else h % 2

    def rs_three(h):
        e = h % 2
        u = landing(h)
        at = axis_one(h)[0]
        _, up, down, far, dp, dm = axis_two(h)
        arrive(r2m[e], "b+", h)
        arrive(r2p[e], "b-", h)
        for name in ("c+", "c-"):
            sent(name, h - 2)

        def body(j, i):
            keep[e][j, i] = (
                partial(h, at, j, i).astype(f32)
                + r2m[e][j, i].astype(f32)
                + r2p[e][j, i].astype(f32)
            ).astype(keep[e].dtype)

        each_tile(body)
        for i in range(tiles_here):
            t1[e][i] = keep[e][far, i].astype(b16)
        if h not in DIRECT_SUMS:
            send(t1[e].at[pl.ds(0, half)], u1[u].at[pl.ds(0, half)], "c+", h, dp)
            send(t1[e].at[pl.ds(half, half)], u1[u].at[pl.ds(half, half)], "c-", h, dm)
            return
        for name in ("d+", "d-"):
            sent(name, h - 2)
        for i in range(tiles_here):
            t2p[e][i] = keep[e][up, i].astype(b16)
            t2m[e][i] = keep[e][down, i].astype(b16)
        send(t2p[e], u2m[u], "d+", h, dp)
        send(t2m[e], u2p[u], "d-", h, dm)
        send(t1[e], u1[u], "c+", h, dev_zo if h % 2 == 0 else dev_xo)

    def rs_four(h):
        e = h % 2
        u = landing(h)
        _, up, down, _, dp, dm = axis_two(h)
        arrive(u1[u].at[pl.ds(0, half)], "c+", h)
        arrive(u1[u].at[pl.ds(half, half)], "c-", h)
        for name in ("d+", "d-"):
            sent(name, h - 2)
        for i in range(tiles_here):
            to_up, to_down = keep[e][up, i].astype(f32), keep[e][down, i].astype(f32)
            if i < half:
                to_up = to_up + u1[u][i].astype(f32)
            else:
                to_down = to_down + u1[u][i].astype(f32)
            t2p[e][i] = to_up.astype(b16)
            t2m[e][i] = to_down.astype(b16)
        send(t2p[e], u2m[u], "d+", h, dp)
        send(t2m[e], u2p[u], "d-", h, dm)

    def rs_five(h):
        e = h % 2
        u = landing(h)
        at = axis_two(h)[0]
        arrive(u2m[u], "d+", h)
        arrive(u2p[u], "d-", h)
        direct = h in DIRECT_SUMS
        if direct:
            arrive(u1[u], "c+", h)
        cols = slice(h * DH, (h + 1) * DH)
        total = keep[e][at].astype(f32) + u2m[u][...].astype(f32) + u2p[u][...].astype(f32)
        if direct:
            total = total + u1[u][...].astype(f32)
        total = total.reshape(tiles_here * block_len, DH)
        hidden = (total * gate_act[:, cols].astype(f32)).astype(b16)
        if not mixed_heads:
            fetched[4].wait()
        for first in range(0, model_width, 2 * DH):
            wide = slice(first, first + 2 * DH)
            product = jnp.dot(hidden, weight[cols, wide], preferred_element_type=f32)
            mixing[:, wide] = mixing[:, wide] + product if mixed_heads else product
        squares[...] = squares[...] + total * total if mixed_heads else total * total
        mixed_heads.append(h)

    mixed_heads = []

    def finish():
        mean_square = jnp.sum(squares[...], axis=1, keepdims=True) * (1.0 / model_width)
        scale = lax.rsqrt(mean_square + norm_epsilon)
        for i in range(tiles_here):
            rows = slice(i * block_len, (i + 1) * block_len)
            mixed_ref[i] = (mixing[rows, :] * scale[rows] + x_in[i].astype(f32)).astype(b16)

    run = {
        "kv_own": kv_own,
        "kv_next": kv_next,
        "kv_far": kv_far,
        "q_own": q_own,
        "q_next": q_next,
        "q_line": q_line,
        "q_line_next": q_line_next,
        "compute0": functools.partial(compute, 0),
        "compute1": functools.partial(compute, 1),
        "compute2": functools.partial(compute, 2),
        "rs_one": rs_one,
        "rs_two": rs_two,
        "rs_three": rs_three,
        "rs_four": rs_four,
        "rs_five": rs_five,
        "route": route,
        "gate_load": gate_load,
        "gate": gate,
    }
    for code in ORDER:
        run[STEPS[code // 8]](code % 8)
    finish()
    for name, h in list(sends):
        sent(name, h)


KEYS = (
    ("kv+", "kv-", "kvf+", "kvf-", "kvs0", "kvs1", "kvs2", "kvs3")
    + ("q+", "q-", "qf+", "qf-", "l+", "l-", "lf+", "lf-")
    + ("a+", "a-", "b+", "b-", "c+", "c-", "d+", "d-")
)


def layer(user_row, hist_len, tile_user, pattern, cand_x, w_query, w_gate, w_out, history):
    tiles_here, block_len, model_width = cand_x.shape
    heads = model_width // DH
    tile_count = tile_user.shape[1]
    cache_rows = CORES * RING * OWN_ROWS
    quads = (tile_count + (QUAD - 1) * cache_rows // 2) // QUAD
    blocks = history.shape[1]
    span = blocks * block_len
    b16 = jnp.bfloat16
    tile = (block_len, DH)
    lines = pltpu.VMEM((RING, tiles_here) + tile, b16)
    half_lines = pltpu.VMEM((RING // 2, tiles_here) + tile, b16)
    few = pltpu.VMEM((tiles_here,) + tile, b16)
    scratch = (
        [pltpu.VMEM((cache_rows * 2 * blocks,) + tile, b16)] * heads
        + [pltpu.VMEM((RING, RING * tiles_here) + tile, b16)] * heads
        + [pltpu.VMEM((quads * QUAD,) + tile, b16)]
        + [lines] * 2
        + [lines] * 4
        + [half_lines] * 4
        + [lines] * 4
        + [lines] * 2
        + [few] * 6
        + [few] * (6 + 3 * len(DIRECT_SUMS))
        + [
            pltpu.VMEM(cand_x.shape, b16),
            pltpu.VMEM(w_query.shape, b16),
            pltpu.VMEM((tiles_here * block_len, model_width), b16),
            pltpu.VMEM((tiles_here * block_len, model_width), jnp.float32),
            pltpu.VMEM((tiles_here * block_len, DH), jnp.float32),
            pltpu.VMEM((tile_count, span), jnp.float32),
            pltpu.VMEM((8, DH), jnp.int32),
            pltpu.SMEM((8, DH), jnp.int32),
            pltpu.SemaphoreType.DMA((heads * OWN_ROWS * 2 + 6,)),
            pltpu.SemaphoreType.DMA((heads * 24,)),
            pltpu.SemaphoreType.DMA((heads * 24,)),
        ]
    )
    smem = pl.BlockSpec(memory_space=pltpu.SMEM)
    vmem = pl.BlockSpec(memory_space=pltpu.VMEM)
    return pl.pallas_call(
        functools.partial(
            layer_kernel,
            heads=heads,
            quads=quads,
            tiles_here=tiles_here,
            block_len=block_len,
            model_width=model_width,
            span=span,
        ),
        in_specs=[smem, smem, vmem, vmem] + [pl.BlockSpec(memory_space=pl.ANY)] * 5,
        out_specs=vmem,
        out_shape=jax.ShapeDtypeStruct(cand_x.shape, b16),
        scratch_shapes=scratch,
        cost_estimate=pl.CostEstimate(
            flops=4 * tile_count * block_len * span * model_width,
            bytes_accessed=2 * history.size,
            transcendentals=tile_count * block_len * span * heads,
        ),
        compiler_params=pltpu.CompilerParams(
            collective_id=0, has_side_effects=True, vmem_limit_bytes=63 * 1024 * 1024
        ),
    )(user_row, hist_len, tile_user, pattern, cand_x, w_query, w_gate, w_out, history)


def per_device(cand_x, w_query, w_gate, w_out, history_kv, tile_user, user_row, hist_len, pattern):
    return layer(
        user_row, hist_len, tile_user[None, :], pattern.T, cand_x, w_query, w_gate, w_out, history_kv
    )


def solution(mesh):
    return jax.shard_map(
        per_device,
        mesh=mesh,
        in_specs=(
            P(("cand", "hist"), None, None),
            P(),
            P(),
            P(),
            P("cand", "hist", None, None),
            P("cand"),
            P(),
            P(),
            P("cand", "hist"),
        ),
        out_specs=P(("cand", "hist"), None, None),
        check_vma=False,
    )
```
